512 devices in a mesh: context: 16 (over z), dp: 8 (over x, core), tensor: 4 (over y).
Axes of the slice: x: 4, y: 4, z: 16, core: 2. Of those that a mesh axis runs over, the one named last changes fastest.
Arguments:
- conv_input: bfloat16 [8, 4096, 4, 2048], P('dp', 'context', None, 'tensor'), may hold values from -6 to 6
- output_grad: bfloat16 [8, 4096, 4, 2048], P('dp', 'context', None, 'tensor'), may hold values from -6 to 6
- b_matrix: bfloat16 [8, 4096, 4, 128], P('dp', 'context'), may hold values from -0.59765625 to 0.59765625
- c_matrix: bfloat16 [8, 4096, 4, 128], P('dp', 'context'), may hold values from -0.59765625 to 0.59765625
- step_size: float32 [8, 4096, 4, 32], P('dp', 'context', None, 'tensor'), may hold values from 0.18 to 5.76, as said below
- decay_rate: float32 [4, 32], P(None, 'tensor'), may hold values from 1e-05 to 0.08
- skip_gain: float32 [4, 32], P(None, 'tensor'), may hold values from 0.5 to 1.5
- conv_weight: float32 [4, 4, 2048], P(None, None, 'tensor'), may hold values from -3 to 3
- conv_bias: float32 [4, 2048], P(None, 'tensor'), may hold values from -3 to 3
- saved_state: bfloat16 [8, 16, 4, 32, 64, 128], P('dp', 'context', None, 'tensor'), may hold values from -0.59765625 to 0.59765625
- doc_lengths: int32 [8, 6], P('dp'), may hold values from 1 to 2048, 4096 in all within a row
Outputs:
- grad_input: bfloat16 [8, 4096, 4, 2048], P('dp', 'context', None, 'tensor')
- grad_b: float32 [8, 4096, 4, 128], P('dp', 'context', 'tensor')
- grad_c: float32 [8, 4096, 4, 128], P('dp', 'context', 'tensor')
- grad_step: float32 [8, 4096, 4, 32], P('dp', 'context', None, 'tensor')
- grad_weight: float32 [4, 4, 2048], P(None, None, 'tensor')
- grad_bias: float32 [4, 2048], P(None, 'tensor')
- grad_rate: float32 [4, 32], P(None, 'tensor')
- grad_skip: float32 [4, 32], P(None, 'tensor')
The draws below stay inside these ranges and needn't reach their ends.
Inputs may be any that keep to these rules, and one draw needn't show every extreme that they name: `step_size`: step sizes vary from position to position and from head to head. `doc_lengths`: the lengths of each row sum to 4096; the longest document of a row has exactly 2048 positions.
All inputs are finite; a program needn't handle non-finite values.
Results may differ from the reference program's by a relative error of at most 0.022.
Values may be sent and summed in bfloat16 or wider, within the bound.
No kernel may reach another device: no remote copies, remote signals or barrier semaphores. Data moves between devices by JAX's collectives and lax.ppermute only.
A program may use at most 128 MiB of HBM per device.

```python
import math
import jax
import jax.numpy as jnp
import numpy as np
from jax import lax

HEAD = 64
STATE = 128
HG = 32
GROUPS = 4
STRETCH = 256
KERNEL = 4
DOCS = 6
PACKED_TOTAL = 8
STRETCHES = 16
PACKED_SPAN = 4096


def head_laws(key, slow_lo, slow_hi, fast_lo, fast_hi, mild_lo, mild_hi, fast_odds):
    key = jax.random.fold_in(key, 101)
    pick_key, slow_key, fast_key, drawn_key, quick_key = jax.random.split(key, 5)
    shape = (GROUPS, HG)
    picked = jax.random.randint(pick_key, shape, 0, 3)
    slow = jnp.exp(jax.random.uniform(slow_key, shape, jnp.float32, math.log(slow_lo), math.log(slow_hi)))
    fast = jnp.exp(jax.random.uniform(fast_key, shape, jnp.float32, math.log(fast_lo), math.log(fast_hi)))
    drawn = jnp.exp(jax.random.uniform(drawn_key, shape, jnp.float32, math.log(mild_lo), math.log(mild_hi)))
    quick = jax.random.randint(quick_key, shape, 0, fast_odds) == 0
    gentle = quick & (picked == 0)
    heavy = jnp.logical_not(quick) & (picked == 1)
    rates = jnp.where(quick, jnp.where(picked == 0, drawn, fast), slow)
    return (rates.astype(jnp.float32), gentle, heavy)


def draw_step_size(key, part):
    rates, gentle, heavy = head_laws(key, 2e-05, 0.006, 0.006, 0.08, 0.006, 0.04, 2)
    key = jax.random.fold_in(key, 11)
    starting_generator, tile_generator, spike_generator, gentle_generator, heavy_generator = jax.random.split(key, 5)
    shape = (PACKED_TOTAL, PACKED_SPAN, GROUPS, HG)
    starting_entropy = jnp.exp(jax.random.uniform(starting_generator, shape, jnp.float32, math.log(0.3), math.log(1.2)))
    tile_entropy = jnp.exp(jax.random.uniform(tile_generator, (PACKED_TOTAL, STRETCHES, GROUPS, HG), jnp.float32, math.log(0.6), math.log(1.6)))
    tile_entropy = jnp.repeat(tile_entropy, STRETCH, axis=1)
    spike_entropy = jax.random.randint(spike_generator, (PACKED_TOTAL, PACKED_SPAN, 1, 1), 0, 512) == 0
    spike_factor = jnp.where(spike_entropy, 3.0, 1.0)
    regular = starting_entropy * tile_entropy * spike_factor
    gentle_rows = jax.random.uniform(gentle_generator, shape, jnp.float32, 0.18, 0.25) * spike_factor
    heavy_rows = jax.random.uniform(heavy_generator, shape, jnp.float32, 2.0, 4.0)
    chosen = jnp.where(gentle[None, None], gentle_rows, jnp.where(heavy[None, None], heavy_rows, regular))
    return chosen.astype(jnp.float32)


def draw_decay_rate(key, part):
    rates, gentle, heavy = head_laws(key, 2e-05, 0.006, 0.006, 0.08, 0.006, 0.04, 2)
    return rates.astype(jnp.float32)


def levels(rng, shape, pieces, low, high):
    loudness = 1.0
    for axis_at, parts in pieces:
        draws = jax.random.uniform(jax.random.fold_in(jax.random.fold_in(rng, 6), axis_at), (parts,), jnp.float32, low / len(pieces), high / len(pieces))
        loudness = loudness * jnp.repeat(jnp.exp(draws), shape[axis_at] // parts).reshape((-1,) + (1,) * (len(shape) - 1 - axis_at))
    return loudness


def length_profile(amount, total, bound, lean):
    weights = [(1 << 20) // math.isqrt(rank ** lean) + 1 for rank in range(2, amount + 1)]
    rest, counts = total - bound - (amount - 1), [1] * (amount - 1)
    while rest > 0:
        free = [i for i in range(amount - 1) if counts[i] < bound]
        mass, budget = sum([weights[i] for i in free]), rest
        for i in free:
            addition = min(bound - counts[i], max(1, budget * weights[i] // mass), rest)
            counts[i] = counts[i] + addition
            rest = rest - addition
    return np.array([bound] + counts)


def uneven_parts(key, amount, total, limit, skew):
    if amount == 2:
        one = jax.random.randint(key, (), max(1, total - limit), min(limit, total - 1) + 1)
        return jnp.stack([one, total - one])
    sizes = jnp.asarray(length_profile(amount, total, limit, skew), jnp.int32)
    twos = (amount - 1) // 2
    donor, receiver = sizes[1:1 + 2 * twos:2], sizes[2:2 + 2 * twos:2]
    margin = jnp.minimum(donor - 1, limit - receiver)
    passed = jax.random.randint(jax.random.fold_in(key, 1), (twos,), 0, 1 << 20) % (margin + 1)
    sizes = sizes.at[1:1 + 2 * twos:2].set(donor - passed).at[2:2 + 2 * twos:2].set(receiver + passed)
    return sizes[jax.random.permutation(jax.random.fold_in(key, 2), amount)]


def scatter_about(stream_key, shape, spread, most, pieces=(), kind=jnp.bfloat16):
    level = levels(stream_key, shape, pieces, -0.22, 0.18) if pieces else 1.0
    result = jax.random.normal(stream_key, shape, jnp.float32) * spread * level
    return jnp.minimum(jnp.maximum(result, -most), most).astype(kind)


def setup_inputs(seed: int = 0) -> dict:
    key_list = jax.random.split(jax.random.key(seed), 12)
    conv_input = scatter_about(key_list[0], (PACKED_TOTAL, PACKED_SPAN, GROUPS, HG * HEAD), 1.0, 6.0, ((0, 8), (1, 16), (3, 4)))
    output_grad = scatter_about(key_list[1], (PACKED_TOTAL, PACKED_SPAN, GROUPS, HG * HEAD), 1.0, 6.0, ((0, 8), (1, 16), (3, 4)))
    b_matrix = scatter_about(key_list[2], (PACKED_TOTAL, PACKED_SPAN, GROUPS, STATE), 0.1, 0.59765625, ((0, 8), (1, 16)))
    c_matrix = scatter_about(key_list[3], (PACKED_TOTAL, PACKED_SPAN, GROUPS, STATE), 0.1, 0.59765625, ((0, 8), (1, 16)))
    step_size = draw_step_size(jax.random.fold_in(key_list[11], 71), 0)
    decay_rate = draw_decay_rate(jax.random.fold_in(key_list[11], 71), 0)
    skip_gain = jnp.clip(0.5 + 1.0 * jax.random.uniform(key_list[6], (GROUPS, HG), jnp.float32) ** levels(key_list[6], (GROUPS, HG), ((1, 4),), -0.2, 0.2), 0.5, 1.5)
    conv_weight = scatter_about(key_list[7], (KERNEL, GROUPS, HG * HEAD), KERNEL ** -0.5, 3.0, ((2, 4),), jnp.float32)
    conv_bias = scatter_about(key_list[8], (GROUPS, HG * HEAD), 0.5, 3.0, ((1, 4),), jnp.float32)
    saved_state = scatter_about(key_list[9], (PACKED_TOTAL, STRETCHES, GROUPS, HG, HEAD, STATE), 0.1, 0.59765625, ((0, 8), (1, 16), (3, 4)))
    doc_lengths = jax.vmap(lambda own: uneven_parts(own, DOCS, PACKED_SPAN, PACKED_SPAN // 2, 2))(jax.random.split(key_list[10], PACKED_TOTAL)).reshape((PACKED_TOTAL, DOCS)).astype(jnp.int32)
    return dict(conv_input=conv_input, output_grad=output_grad, b_matrix=b_matrix, c_matrix=c_matrix, step_size=step_size, decay_rate=decay_rate, skip_gain=skip_gain, conv_weight=conv_weight, conv_bias=conv_bias, saved_state=saved_state, doc_lengths=doc_lengths)


exact_prec = lax.Precision.HIGHEST

def mixed(form, left, right):
    return jnp.einsum(form, left.astype(jnp.float32), right.astype(jnp.float32), precision=exact_prec)

def segment_ids(doc_lengths, positions):
    starts = jnp.cumsum(doc_lengths, axis=-1) - doc_lengths
    before = starts[:, None, :] <= positions[None, :, None]
    return lax.optimization_barrier(jnp.sum(before.astype(jnp.int32), axis=-1)).astype(jnp.int32)

def conv_forward(extended, seg_ext, conv_weight, conv_bias):
    kernel_width = conv_weight.shape[0]
    row_count = extended.shape[1] - kernel_width + 1
    seg_now = seg_ext[:, kernel_width - 1:]
    summed = jnp.zeros(extended[:, kernel_width - 1:].shape, jnp.float32) + conv_bias
    for lag_index in range(kernel_width):
        first_row = kernel_width - 1 - lag_index
        window_rows = extended[:, first_row:first_row + row_count].astype(jnp.float32)
        same_doc = (seg_ext[:, first_row:first_row + row_count] == seg_now)[:, :, None, None]
        summed = summed + jnp.where(same_doc, conv_weight[lag_index] * window_rows, 0.0)
    return summed

def conv_input_grad(grad_ext, seg_ext, conv_weight):
    kernel_width = conv_weight.shape[0]
    row_count = grad_ext.shape[1] - kernel_width + 1
    seg_now = seg_ext[:, :row_count]
    summed = jnp.zeros(grad_ext[:, :row_count].shape, jnp.float32)
    for lag_index in range(kernel_width):
        window_rows = grad_ext[:, lag_index:lag_index + row_count]
        same_doc = (seg_ext[:, lag_index:lag_index + row_count] == seg_now)[:, :, None, None]
        summed = summed + jnp.where(same_doc, conv_weight[lag_index] * window_rows, 0.0)
    return summed

def conv_weight_grad(extended, seg_ext, grad_pre):
    kernel_width = extended.shape[1] - grad_pre.shape[1] + 1
    row_count = grad_pre.shape[1]
    seg_now = seg_ext[:, kernel_width - 1:]
    lag_terms = []
    for lag_index in range(kernel_width):
        first_row = kernel_width - 1 - lag_index
        window_rows = extended[:, first_row:first_row + row_count].astype(jnp.float32)
        same_doc = (seg_ext[:, first_row:first_row + row_count] == seg_now)[:, :, None, None]
        lag_terms.append(lax.optimization_barrier(jnp.sum(jnp.where(same_doc, grad_pre * window_rows, 0.0), axis=(0, 1))))
    return jnp.stack(lag_terms)

def lower_ones(row_count):
    row_index = jnp.arange(row_count)
    return (row_index[:, None] >= row_index[None, :]).astype(jnp.float32)

def decay_terms(step_size, decay_rate, segment, segment_before):
    row_count = step_size.shape[1]
    log_decay = -step_size * decay_rate
    cumulative = jnp.einsum('ts,bsgk->btgk', lower_ones(row_count), log_decay, precision=exact_prec)
    alive = (segment == segment_before[:, None])[:, :, None, None]
    from_start = jnp.where(alive, jnp.exp(cumulative), 0.0)
    through = from_start[:, -1]
    same_end = (segment == segment[:, -1:])[:, :, None, None]
    to_end = jnp.where(same_end, jnp.exp(jnp.minimum(cumulative[:, -1:] - cumulative, 0.0)), 0.0)
    return (cumulative, from_start, to_end, through)

def group_intra(update, grad_y, b_group, c_group, cumulative, from_start, start_state, segment):
    row_count = cumulative.shape[1]
    row_index = jnp.arange(row_count)
    causal = row_index[:, None] >= row_index[None, :]
    same_doc = causal[None] & (segment[:, :, None] == segment[:, None, :])
    cum_heads = jnp.moveaxis(cumulative, 2, 1)
    log_gaps = cum_heads[:, :, :, None] - cum_heads[:, :, None, :]
    decay_mask = jnp.where(same_doc[:, None], jnp.exp(jnp.minimum(log_gaps, 0.0)), 0.0)
    gram_matrix = mixed('btn,bsn->bts', c_group, b_group)
    scores = decay_mask * gram_matrix[:, None]
    score_bf = scores.astype(jnp.bfloat16)
    grad_update = mixed('bkts,btkp->bskp', score_bf, grad_y)
    grad_score = mixed('btkp,bskp->bkts', grad_y, update)
    product = scores * grad_score
    grad_cum = lax.optimization_barrier(jnp.sum(product, axis=3)) - lax.optimization_barrier(jnp.sum(product, axis=2))
    grad_gram = lax.optimization_barrier(jnp.sum(decay_mask * grad_score, axis=1)).astype(jnp.bfloat16)
    grad_c = mixed('bts,bsn->btn', grad_gram, b_group)
    grad_b = mixed('bts,btn->bsn', grad_gram, c_group)
    state_c = mixed('bkpn,btn->btkp', start_state, c_group)
    grad_cum = jnp.moveaxis(grad_cum, 1, 2) + from_start * lax.optimization_barrier(jnp.sum(grad_y.astype(jnp.float32) * state_c, axis=-1))
    grad_state = mixed('btkp,bkpn->btkn', grad_y, start_state)
    grad_c = grad_c + lax.optimization_barrier(jnp.sum(from_start[..., None] * grad_state, axis=2))
    scaled_grad = (from_start[..., None] * grad_y.astype(jnp.float32)).astype(jnp.bfloat16)
    offset = mixed('btkp,btn->bkpn', scaled_grad, c_group)
    return (grad_update, grad_cum, grad_c, grad_b, offset)

def group_carry(state_grad, update, b_group, to_end, start_state, through):
    state_bf = state_grad.astype(jnp.bfloat16)
    carry_b = mixed('bkpn,bsn->bskp', state_bf, b_group)
    grad_update = to_end[..., None] * carry_b
    along_end = to_end * lax.optimization_barrier(jnp.sum(update.astype(jnp.float32) * carry_b, axis=-1))
    update_carry = mixed('bskp,bkpn->bskn', update, state_bf)
    grad_b = lax.optimization_barrier(jnp.sum(to_end[..., None] * update_carry, axis=2))
    last_term = lax.optimization_barrier(jnp.sum(along_end, axis=1)) + through * lax.optimization_barrier(jnp.sum(state_grad * start_state.astype(jnp.float32), axis=(2, 3)))
    row_count = along_end.shape[1]
    is_last = (jnp.arange(row_count) == row_count - 1)[None, :, None]
    grad_cum = jnp.where(is_last, last_term[:, None, :], 0.0) - along_end
    return (grad_update, grad_cum, grad_b)

def stretch_intra(update, grad_y, b_matrix, c_matrix, cumulative, from_start, start_state, segment):

    def one_group(group_items):
        return group_intra(*group_items, segment)
    results = lax.map(one_group, (jnp.moveaxis(update, 2, 0), jnp.moveaxis(grad_y, 2, 0), jnp.moveaxis(b_matrix, 2, 0), jnp.moveaxis(c_matrix, 2, 0), jnp.moveaxis(cumulative, 2, 0), jnp.moveaxis(from_start, 2, 0), jnp.moveaxis(start_state, 1, 0)))
    return (jnp.moveaxis(results[0], 0, 2), jnp.moveaxis(results[1], 0, 2), jnp.moveaxis(results[2], 0, 2), jnp.moveaxis(results[3], 0, 2), jnp.moveaxis(results[4], 0, 1))

def stretch_carry(state_grad, update, b_matrix, to_end, start_state, through):

    def one_group(group_items):
        return group_carry(*group_items)
    results = lax.map(one_group, (jnp.moveaxis(state_grad, 1, 0), jnp.moveaxis(update, 2, 0), jnp.moveaxis(b_matrix, 2, 0), jnp.moveaxis(to_end, 2, 0), jnp.moveaxis(start_state, 1, 0), jnp.moveaxis(through, 1, 0)))
    return (jnp.moveaxis(results[0], 0, 2), jnp.moveaxis(results[1], 0, 2), jnp.moveaxis(results[2], 0, 2))

def finish(grad_update, grad_cum, step_size, conv_heads, grad_y, decay_rate, skip_gain):
    row_count = grad_cum.shape[1]
    grad_log = jnp.einsum('ts,btgk->bsgk', lower_ones(row_count), grad_cum, precision=exact_prec)
    grad_step = -decay_rate * grad_log + lax.optimization_barrier(jnp.sum(grad_update * conv_heads.astype(jnp.float32), axis=-1))
    grad_conv = step_size[..., None] * grad_update + skip_gain[..., None] * grad_y.astype(jnp.float32)
    grad_rate = -lax.optimization_barrier(jnp.sum(step_size * grad_log, axis=(0, 1)))
    grad_skip = lax.optimization_barrier(jnp.sum(lax.optimization_barrier(jnp.sum(grad_y.astype(jnp.float32) * conv_heads.astype(jnp.float32), axis=-1)), axis=(0, 1)))
    return (grad_step, grad_conv, grad_rate, grad_skip)

def reference(conv_input, output_grad, b_matrix, c_matrix, step_size, decay_rate, skip_gain, conv_weight, conv_bias, saved_state, doc_lengths):
    seq_count, total_rows, groups, features = conv_input.shape
    kernel_width = conv_weight.shape[0]
    head_count = step_size.shape[3]
    head_dim = features // head_count
    stretches = total_rows // STRETCH
    positions = jnp.arange(-(kernel_width - 1), total_rows + kernel_width - 1).astype(jnp.int32)
    seg_all = segment_ids(doc_lengths, positions)
    seg_before = seg_all[:, :total_rows + kernel_width - 1]
    seg_here = seg_all[:, kernel_width - 1:kernel_width - 1 + total_rows]
    seg_after = seg_all[:, kernel_width - 1:]
    extended = jnp.concatenate([jnp.zeros((seq_count, kernel_width - 1, groups, features), conv_input.dtype), conv_input], axis=1)
    pre_act = conv_forward(extended, seg_before, conv_weight, conv_bias)
    conv_out = jax.nn.silu(pre_act).astype(jnp.bfloat16)
    conv_heads = conv_out.reshape(seq_count, total_rows, groups, head_count, head_dim)
    grad_heads = output_grad.reshape(seq_count, total_rows, groups, head_count, head_dim)
    update = (step_size[..., None] * conv_heads.astype(jnp.float32)).astype(jnp.bfloat16)

    def blocks(array):
        return jnp.moveaxis(array.reshape((seq_count, stretches, STRETCH) + array.shape[2:]), 1, 0)

    def unblock(array):
        return jnp.moveaxis(array, 0, 1).reshape((seq_count, total_rows) + array.shape[3:])
    seg_first = jnp.moveaxis(seg_all[:, kernel_width - 2:kernel_width - 2 + total_rows:STRETCH], 1, 0)
    states = jnp.moveaxis(saved_state, 1, 0)

    def per_stretch(state_grad, stretch_items):
        upd_rows, grad_rows, b_rows, c_rows, step_rows, conv_rows, segment, segment_before, start_state = stretch_items
        cumulative, from_start, to_end, through = decay_terms(step_rows, decay_rate, segment, segment_before)
        update_one, cum_one, grad_c, b_one, offset = stretch_intra(upd_rows, grad_rows, b_rows, c_rows, cumulative, from_start, start_state, segment)
        update_two, cum_two, b_two = stretch_carry(state_grad, upd_rows, b_rows, to_end, start_state, through)
        grad_step, grad_conv, grad_rate, grad_skip = finish(update_one + update_two, cum_one + cum_two, step_rows, conv_rows, grad_rows, decay_rate, skip_gain)
        next_grad = through[..., None, None] * state_grad + offset
        return (next_grad, (grad_step, grad_conv, grad_c, b_one + b_two, grad_rate, grad_skip))
    initial = jnp.zeros((seq_count, groups, head_count, head_dim, STATE), jnp.float32)
    _, results = lax.scan(per_stretch, initial, (blocks(update), blocks(grad_heads), blocks(b_matrix), blocks(c_matrix), blocks(step_size), blocks(conv_heads), blocks(seg_here), seg_first, states), reverse=True)
    grad_step = unblock(results[0])
    grad_conv = unblock(results[1]).reshape(seq_count, total_rows, groups, features)
    grad_c = unblock(results[2])
    grad_b = unblock(results[3])
    grad_rate = lax.optimization_barrier(jnp.sum(results[4], axis=0))
    grad_skip = lax.optimization_barrier(jnp.sum(results[5], axis=0))
    sigmoid_pre = jax.nn.sigmoid(pre_act)
    grad_pre = grad_conv * (sigmoid_pre * (1.0 + pre_act * (1.0 - sigmoid_pre)))
    grad_ext = jnp.concatenate([grad_pre, jnp.zeros((seq_count, kernel_width - 1, groups, features), jnp.float32)], axis=1)
    grad_input = conv_input_grad(grad_ext, seg_after, conv_weight).astype(jnp.bfloat16)
    grad_weight = conv_weight_grad(extended, seg_before, grad_pre)
    grad_bias = lax.optimization_barrier(jnp.sum(grad_pre, axis=(0, 1)))
    return (grad_input, grad_b, grad_c, grad_step, grad_weight, grad_bias, grad_rate, grad_skip)
```

```python
import jax
import jax.numpy as jnp
from jax import lax
from jax.experimental import pallas as pl
from jax.experimental.pallas import tpu as pltpu
from jax.sharding import PartitionSpec as P

F32 = jnp.float32
BF16 = jnp.bfloat16
LOG2E = 1.4426950408889634
FULL = lax.Precision.HIGHEST
HEAD = 64
HALO = 8
EXTRA = 16
FAR = 1 << 28


def dot(a, b, dims=((1,), (0,)), precision=None):
    return lax.dot_general(a, b, (dims, ((), ())), precision=precision, preferred_element_type=F32)


NT = ((1,), (1,))
TN = ((0,), (0,))


def iota(shape, axis):
    return lax.broadcasted_iota(jnp.int32, shape, axis)


def doc_bounds(first, lengths, rows):
    pos = first + iota((1, rows), 1)
    low = jnp.zeros((1, rows), jnp.int32)
    high = jnp.full((1, rows), FAR, jnp.int32)
    start = jnp.int32(0)
    for d in range(lengths.shape[1]):
        low = jnp.where(pos >= start, start, low)
        start = start + lengths[0, d]
        high = jnp.minimum(high, jnp.where(start > pos, start - 1, FAR))
    return low, high


def per_head(values, group, shape):
    column = jnp.zeros(shape, F32)
    for h in range(shape[0]):
        column = jnp.where(iota(shape, 0) == h, values[group, h], column)
    return column


def running_log(step, rate):
    rows = step.shape[1]
    upto = (iota((rows, rows), 0) <= iota((rows, rows), 1)).astype(F32)
    return dot(step * (rate * (-LOG2E)), upto, precision=FULL)


def offset_kernel(first, lengths, rate, step, gy, cm, pay, gyt, rows_out):
    g = pl.program_id(0)
    rows = step.shape[2]
    heads = step.shape[1]
    low, high = doc_bounds(first[0], lengths, rows)
    cum = running_log(step[0], per_head(rate, g, (heads, rows)))
    from_start = jnp.where(low < first[0], jnp.exp2(cum), 0.0)
    last = jnp.broadcast_to(cum[:, rows - 1 :], (heads, rows))
    to_end = jnp.where(high >= first[0] + rows - 1, jnp.exp2(jnp.minimum(last - cum, 0.0)), 0.0)
    rows_out[0, 0] = cum
    rows_out[0, 1] = from_start
    rows_out[0, 2] = to_end
    gt = jnp.transpose(gy[0].astype(F32))
    gyt[0] = gt.astype(BF16)
    scaled = jnp.concatenate(
        [gt[h * HEAD : (h + 1) * HEAD] * from_start[h : h + 1] for h in range(heads)], axis=0
    ).astype(BF16)
    offset = dot(scaled, cm[0]).astype(BF16)
    through = jnp.broadcast_to(from_start[:, rows - 1 :], (heads, 128))
    upper = through.astype(BF16).astype(F32)
    lower = through - upper
    spot = iota((EXTRA, 128), 0)
    for e in range(heads // 2):
        pay[e, : 2 * HEAD] = offset[e * 2 * HEAD : (e + 1) * 2 * HEAD]
        extra = jnp.where(spot == 0, upper[2 * e : 2 * e + 1], 0.0)
        extra = jnp.where(spot == 1, lower[2 * e : 2 * e + 1], extra)
        extra = jnp.where(spot == 2, upper[2 * e + 1 : 2 * e + 2], extra)
        extra = jnp.where(spot == 3, lower[2 * e + 1 : 2 * e + 2], extra)
        pay[e, 2 * HEAD :] = extra.astype(BF16)


def scan_kernel(pay, out):
    blocks = pay.shape[0]
    state = jnp.zeros((2 * HEAD, 128), F32)
    out[blocks - 1] = state.astype(BF16)
    for k in range(blocks - 2, -1, -1):
        extra = pay[k + 1, 2 * HEAD :].astype(F32)
        one = jnp.broadcast_to(extra[0:1] + extra[1:2], (HEAD, 128))
        two = jnp.broadcast_to(extra[2:3] + extra[3:4], (HEAD, 128))
        through = jnp.concatenate([one, two], axis=0)
        state = through * state + pay[k + 1, : 2 * HEAD].astype(F32)
        out[k] = state.astype(BF16)


def intra_kernel(
    first, lengths, skip, x, halo, gy, gyt, bm, cm, step, rows_in, state, taps,
    lagged, conv, upd, slope, part, heads_out, gc, gb, acc, statec,
):
    g = pl.program_id(0)
    heads = step.shape[1]
    rows = step.shape[2]
    start = first[0]
    low, high = doc_bounds(start, lengths, rows)
    sub = iota((rows, rows), 0)
    lane = iota((rows, rows), 1)
    xt = jnp.transpose(x[0].astype(F32)).astype(BF16)
    lagged[0, 0] = xt
    hsub = iota((HALO, rows), 0)
    hlane = iota((HALO, rows), 1)
    for j in range(1, 4):
        here = ((sub + j == lane) & (sub + start >= low)).astype(BF16)
        away = ((hsub - HALO + j == hlane) & (hsub - HALO + start >= low)).astype(BF16)
        lagged[0, j] = (dot(xt, here) + dot(halo[0], away, TN)).astype(BF16)
    statec[...] = dot(state[0], cm[0], NT)
    gram = dot(cm[0], bm[0], NT)
    bias = jnp.where((sub >= lane) & (sub + start <= high), 0.0, -1e30)
    cum = rows_in[0, 0]
    cum_col = jnp.transpose(cum)
    acc[...] = jnp.zeros((rows, rows), F32)
    zero = jnp.zeros((HEAD, rows), BF16)
    spot = iota((heads, rows), 0)
    cum_out = jnp.zeros((heads, rows), F32)
    step_out = jnp.zeros((heads, rows), F32)
    skip_out = jnp.zeros((heads, rows), F32)
    for h in range(heads):
        at = slice(h * HEAD, (h + 1) * HEAD)
        w = taps[0, at]
        pre = w[:, 4:5] + w[:, 0:1] * lagged[0, 0, at].astype(F32)
        for j in range(1, 4):
            pre = pre + w[:, j : j + 1] * lagged[0, j, at].astype(F32)
        sig = 1.0 / (1.0 + jnp.exp(-pre))
        co = (pre * sig).astype(BF16)
        conv[0, at] = co
        slope[0, at] = sig * (1.0 + pre * (1.0 - sig))
        co = co.astype(F32)
        st = step[0, h : h + 1]
        u = (st * co).astype(BF16)
        upd[0, at] = u
        pair = gy[0, :, (h // 2) * 128 : (h // 2 + 1) * 128]
        both = jnp.concatenate([u, zero] if h % 2 == 0 else [zero, u], axis=0)
        score_grad = dot(pair, both)
        decay = jnp.exp2(cum_col[:, h : h + 1] - cum[h : h + 1] + bias)
        acc[...] += decay * score_grad
        score = (decay * gram).astype(BF16)
        gt = gyt[0, at]
        grad_u = dot(gt, score)
        y = dot(u, score, NT)
        gt = gt.astype(F32)
        row_sum = jnp.sum(gt * (y + rows_in[0, 1, h : h + 1] * statec[at]), axis=0, keepdims=True)
        col_sum = jnp.sum(u.astype(F32) * grad_u, axis=0, keepdims=True)
        cum_out = jnp.where(spot == h, row_sum - col_sum, cum_out)
        step_out = jnp.where(spot == h, jnp.sum(grad_u * co, axis=0, keepdims=True), step_out)
        skip_out = jnp.where(spot == h, jnp.sum(gt * co, axis=0, keepdims=True), skip_out)
        part[0, at] = st * grad_u + skip[g, h] * gt
    heads_out[0, 0] = cum_out
    heads_out[0, 1] = step_out
    heads_out[0, 2] = skip_out
    grad_gram = acc[...].astype(BF16)
    scaled = jnp.concatenate(
        [
            (gyt[0, h * HEAD : (h + 1) * HEAD].astype(F32) * rows_in[0, 1, h : h + 1]).astype(BF16)
            for h in range(heads)
        ],
        axis=0,
    )
    gc[0] = (dot(grad_gram, bm[0]) + dot(scaled, state[0], TN)).astype(BF16)
    gb[0] = dot(grad_gram, cm[0], TN)


def carry_kernel(
    rate, grad, bm, step, rows_in, heads_in, state, lagged, conv, slope, part,
    pay, grad_step, pre_out, edge, cols,
):
    g = pl.program_id(0)
    heads = step.shape[1]
    rows = step.shape[2]
    carry = dot(grad[0], bm[0], NT)
    spot = iota((heads, rows), 0)
    lane = iota((HEAD, 128), 1)
    to_end = rows_in[0, 2]
    along = jnp.zeros((heads, rows), F32)
    inner = jnp.zeros((heads, 128), F32)
    for h in range(heads):
        at = slice(h * HEAD, (h + 1) * HEAD)
        cb = carry[at]
        st = step[0, h : h + 1]
        along = jnp.where(spot == h, jnp.sum(cb * conv[0, at].astype(F32), axis=0, keepdims=True), along)
        prod = grad[0, at].astype(F32) * state[0, at].astype(F32)
        inner = jnp.where(
            iota((heads, 128), 0) == h, jnp.sum(prod, axis=0, keepdims=True), inner
        )
        gp = (part[0, at] + (st * to_end[h : h + 1]) * cb) * slope[0, at]
        pre_out[0, at] = gp.astype(BF16)
        out = jnp.where(lane == 12, jnp.sum(gp, axis=1, keepdims=True), gp[:, :128])
        for j in range(4):
            s = jnp.sum(gp * lagged[0, j, at].astype(F32), axis=1, keepdims=True)
            out = jnp.where(lane == 8 + j, s, out)
        cols[at] = out
    along = along * to_end
    step_two = along
    along = along * step[0]
    through = rows_in[0, 1][:, rows - 1 :]
    last = jnp.sum(along, axis=1, keepdims=True) + through * jnp.sum(inner, axis=1, keepdims=True)
    grad_cum = heads_in[0, 0] - along + jnp.where(iota((heads, rows), 1) == rows - 1, last, 0.0)
    back = (iota((rows, rows), 0) >= iota((rows, rows), 1)).astype(F32)
    grad_log = dot(grad_cum, back, precision=FULL)
    grad_step[0] = heads_in[0, 1] + step_two - per_head(rate, g, (heads, rows)) * grad_log
    lane = iota((heads, 128), 1)
    rate_grad = -jnp.sum(step[0] * grad_log, axis=1, keepdims=True)
    skip_grad = jnp.sum(heads_in[0, 2], axis=1, keepdims=True)
    top = cols[:heads]
    top = jnp.where(lane == 13, rate_grad, top)
    cols[:heads] = jnp.where(lane == 14, skip_grad, top)
    turned = jnp.transpose(cols[...])
    edge[0] = turned[:HALO].astype(BF16)
    pay[0] = turned[8:16]


def grad_b_kernel(rows_in, upd, grad, gb, out):
    heads = rows_in.shape[2]
    scaled = jnp.concatenate(
        [
            (upd[0, h * HEAD : (h + 1) * HEAD].astype(F32) * rows_in[0, 2, h : h + 1]).astype(BF16)
            for h in range(heads)
        ],
        axis=0,
    )
    out[0] = (gb[0] + dot(scaled, grad[0], TN)).astype(BF16)


def input_kernel(first, lengths, pre, right, taps, out):
    rows = pre.shape[2]
    start = first[0]
    _, high = doc_bounds(start, lengths, rows)
    sub = iota((rows, rows), 0)
    lane = iota((rows, rows), 1)
    hsub = iota((HALO, rows), 0)
    hlane = iota((HALO, rows), 1)
    w = taps[0]
    total = w[:, 0:1] * pre[0].astype(F32)
    for j in range(1, 4):
        here = ((sub == lane + j) & (sub + start <= high)).astype(BF16)
        away = ((hsub + rows == hlane + j) & (hsub + rows + start <= high)).astype(BF16)
        total = total + w[:, j : j + 1] * (dot(pre[0], here) + dot(right[0], away, TN))
    out[0] = jnp.transpose(total).astype(BF16)


def sum_kernel(parts, out):
    total = parts[0].astype(F32)
    for i in range(1, parts.shape[0]):
        total = total + parts[i].astype(F32)
    out[...] = total.astype(out.dtype)


def call(kernel, grid, ins, outs, args, flops=0, nbytes=0, scratch=()):
    smem = pl.BlockSpec(memory_space=pltpu.SMEM)

    def spec(shape, blocked):
        if blocked is None:
            return smem
        if not blocked or not grid:
            return pl.BlockSpec(shape, lambda *i: (0,) * len(shape))
        return pl.BlockSpec(
            (shape[0] // grid[0],) + tuple(shape[1:]), lambda g: (g,) + (0,) * (len(shape) - 1)
        )

    return pl.pallas_call(
        kernel,
        grid=grid,
        in_specs=[spec(a.shape, b) for a, b in zip(args, ins)],
        out_specs=[spec(s, True) for s, _ in outs],
        out_shape=[jax.ShapeDtypeStruct(s, t) for s, t in outs],
        scratch_shapes=list(scratch),
        cost_estimate=pl.CostEstimate(flops=flops, bytes_accessed=nbytes, transcendentals=0),
        compiler_params=pltpu.CompilerParams(vmem_limit_bytes=48 * 1024 * 1024),
    )(*args)


def shifted(block, axis, distance):
    size = lax.axis_size(axis)
    route = [(i, i + distance) for i in range(size) if 0 <= i + distance < size]
    return lax.ppermute(block, axis, route)


def body(
    conv_input,
    output_grad,
    b_matrix,
    c_matrix,
    step_size,
    decay_rate,
    skip_gain,
    conv_weight,
    conv_bias,
    saved_state,
    doc_lengths,
):
    _, rows, groups, features = conv_input.shape
    heads = step_size.shape[3]
    blocks = lax.axis_size("context")
    first = (lax.axis_index("context") * rows).astype(jnp.int32).reshape(1)
    x = jnp.transpose(conv_input[0], (1, 0, 2))
    gy = jnp.transpose(output_grad[0], (1, 0, 2))
    bm = jnp.transpose(b_matrix[0], (1, 0, 2))
    cm = jnp.transpose(c_matrix[0], (1, 0, 2))
    step = jnp.transpose(step_size[0], (1, 2, 0))
    state = saved_state.reshape(groups, features, 128)
    taps = jnp.concatenate(
        [
            jnp.transpose(conv_weight, (1, 2, 0)),
            conv_bias[:, :, None],
            jnp.zeros((groups, features, 3), F32),
        ],
        axis=2,
    )
    halo = shifted(conv_input[0, rows - HALO :], "context", 1)
    halo = jnp.transpose(halo, (1, 0, 2))

    wide = (groups, features, rows)
    pay, gyt, rows_in = call(
        offset_kernel,
        (groups,),
        [None, None, None, True, True, True],
        [
            ((groups * heads // 2, 2 * HEAD + EXTRA, 128), BF16),
            (wide, BF16),
            ((groups, 3, heads, rows), F32),
        ],
        (first, doc_lengths, decay_rate, step, gy, cm),
        flops=10**9,
        nbytes=4 * 10**6,
    )
    own = groups * heads // 2 // blocks
    gathered = lax.all_to_all(pay, "context", 0, 0, tiled=True)
    lagged, conv, upd, slope, part, heads_in, gc, gb = call(
        intra_kernel,
        (groups,),
        [None, None, None] + [True] * 10,
        [
            ((groups, 4, features, rows), BF16),
            (wide, BF16),
            (wide, BF16),
            (wide, F32),
            (wide, F32),
            ((groups, 3, heads, rows), F32),
            ((groups, rows, 128), BF16),
            ((groups, rows, 128), F32),
        ],
        (first, doc_lengths, skip_gain, x, halo, gy, gyt, bm, cm, step, rows_in, state, taps),
        flops=20 * 10**9,
        nbytes=20 * 10**6,
        scratch=(pltpu.VMEM((rows, rows), F32), pltpu.VMEM((features, rows), F32)),
    )
    (scanned,) = call(
        scan_kernel,
        (),
        [True],
        [((blocks * own, 2 * HEAD, 128), BF16)],
        (gathered,),
        flops=10**7,
        nbytes=10**6,
    )
    grad = lax.all_to_all(scanned, "context", 0, 0, tiled=True).reshape(groups, features, 128)
    grad_c = lax.psum_scatter(gc, "tensor", scatter_dimension=0, tiled=True).astype(F32)
    sums, grad_step, pre, edge = call(
        carry_kernel,
        (groups,),
        [None] + [True] * 10,
        [
            ((groups, 8, features), F32),
            ((groups, heads, rows), F32),
            (wide, BF16),
            ((groups, HALO, features), BF16),
        ],
        (decay_rate, grad, bm, step, rows_in, heads_in, state, lagged, conv, slope, part),
        flops=10**9,
        nbytes=20 * 10**6,
        scratch=(pltpu.VMEM((features, 128), F32),),
    )
    copies = lax.axis_size("dp")
    shares = jnp.broadcast_to(sums.astype(BF16)[None], (copies,) + sums.shape)
    shares = lax.all_to_all(shares, "dp", 0, 0, tiled=True)
    (sums,) = call(sum_kernel, (), [True], [(sums.shape, BF16)], (shares,))
    shares = jnp.broadcast_to(sums[None], (blocks,) + sums.shape)
    shares = lax.all_to_all(shares, "context", 0, 0, tiled=True)
    (sums,) = call(sum_kernel, (), [True], [(sums.shape, F32)], (shares,))

    (gb,) = call(
        grad_b_kernel,
        (groups,),
        [True] * 4,
        [((groups, rows, 128), BF16)],
        (rows_in, upd, grad, gb),
        flops=10**8,
        nbytes=2 * 10**6,
    )
    parts = lax.axis_size("tensor")
    here = groups // parts
    gb = lax.all_to_all(gb, "tensor", 0, 0, tiled=True).reshape(parts, here * rows, 128)
    (grad_b,) = call(sum_kernel, (), [True], [((here * rows, 128), F32)], (gb,))

    right = shifted(edge, "context", -1)
    (grad_input,) = call(
        input_kernel,
        (groups,),
        [None, None] + [True] * 3,
        [((groups, rows, features), BF16)],
        (first, doc_lengths, pre, right, taps),
        flops=10**9,
        nbytes=4 * 10**6,
    )
    return (
        jnp.transpose(grad_input, (1, 0, 2))[None],
        jnp.transpose(grad_b.reshape(1, here, rows, 128), (0, 2, 1, 3)),
        jnp.transpose(grad_c.reshape(1, here, rows, 128), (0, 2, 1, 3)),
        jnp.transpose(grad_step, (2, 0, 1))[None],
        jnp.transpose(sums[:, :4], (1, 0, 2)),
        sums[:, 4],
        sums[:, 5, :heads],
        sums[:, 6, :heads],
    )


def solution(mesh):
    return jax.shard_map(
        body,
        mesh=mesh,
        in_specs=(
            P("dp", "context", None, "tensor"),
            P("dp", "context", None, "tensor"),
            P("dp", "context", None, None),
            P("dp", "context", None, None),
            P("dp", "context", None, "tensor"),
            P(None, "tensor"),
            P(None, "tensor"),
            P(None, None, "tensor"),
            P(None, "tensor"),
            P("dp", "context", None, "tensor", None, None),
            P("dp", None),
        ),
        out_specs=(
            P("dp", "context", None, "tensor"),
            P("dp", "context", "tensor", None),
            P("dp", "context", "tensor", None),
            P("dp", "context", None, "tensor"),
            P(None, None, "tensor"),
            P(None, "tensor"),
            P(None, "tensor"),
            P(None, "tensor"),
        ),
        check_vma=False,
    )
```

```python
import jax
import jax.numpy as jnp
from jax import lax
from jax.experimental import pallas as pl
from jax.experimental.pallas import tpu as pltpu
from jax.sharding import PartitionSpec as P

F32 = jnp.float32
BF16 = jnp.bfloat16
LOG2E = 1.4426950408889634
FULL = lax.Precision.HIGHEST
HEAD = 64
HALO = 8
EXTRA = 16
FAR = 1 << 28


def dot(a, b, dims=((1,), (0,)), precision=None):
    return lax.dot_general(a, b, (dims, ((), ())), precision=precision, preferred_element_type=F32)


NT = ((1,), (1,))
TN = ((0,), (0,))


def iota(shape, axis):
    return lax.broadcasted_iota(jnp.int32, shape, axis)


def doc_bounds(first, lengths, rows):
    pos = first + iota((1, rows), 1)
    low = jnp.zeros((1, rows), jnp.int32)
    high = jnp.full((1, rows), FAR, jnp.int32)
    start = jnp.int32(0)
    for d in range(lengths.shape[1]):
        low = jnp.where(pos >= start, start, low)
        start = start + lengths[0, d]
        high = jnp.minimum(high, jnp.where(start > pos, start - 1, FAR))
    return low, high


def per_head(values, group, shape):
    column = jnp.zeros(shape, F32)
    for h in range(shape[0]):
        column = jnp.where(iota(shape, 0) == h, values[group, h], column)
    return column


def running_log(step, rate):
    rows = step.shape[1]
    upto = (iota((rows, rows), 0) <= iota((rows, rows), 1)).astype(F32)
    return dot(step * (rate * (-LOG2E)), upto, precision=FULL)


def offset_kernel(first, lengths, rate, step, gy, cm, pay, gyt, rows_out):
    g = pl.program_id(0)
    rows = step.shape[2]
    heads = step.shape[1]
    low, high = doc_bounds(first[0], lengths, rows)
    cum = running_log(step[0], per_head(rate, g, (heads, rows)))
    from_start = jnp.where(low < first[0], jnp.exp2(cum), 0.0)
    last = jnp.broadcast_to(cum[:, rows - 1 :], (heads, rows))
    to_end = jnp.where(high >= first[0] + rows - 1, jnp.exp2(jnp.minimum(last - cum, 0.0)), 0.0)
    rows_out[0, 0] = cum
    rows_out[0, 1] = from_start
    rows_out[0, 2] = to_end
    gt = jnp.transpose(gy[0].astype(F32))
    gyt[0] = gt.astype(BF16)
    scaled = jnp.concatenate(
        [gt[h * HEAD : (h + 1) * HEAD] * from_start[h : h + 1] for h in range(heads)], axis=0
    ).astype(BF16)
    offset = dot(scaled, cm[0]).astype(BF16)
    through = jnp.broadcast_to(from_start[:, rows - 1 :], (heads, 128))
    upper = through.astype(BF16).astype(F32)
    lower = through - upper
    spot = iota((EXTRA, 128), 0)
    for e in range(heads // 2):
        pay[e, : 2 * HEAD] = offset[e * 2 * HEAD : (e + 1) * 2 * HEAD]
        extra = jnp.where(spot == 0, upper[2 * e : 2 * e + 1], 0.0)
        extra = jnp.where(spot == 1, lower[2 * e : 2 * e + 1], extra)
        extra = jnp.where(spot == 2, upper[2 * e + 1 : 2 * e + 2], extra)
        extra = jnp.where(spot == 3, lower[2 * e + 1 : 2 * e + 2], extra)
        pay[e, 2 * HEAD :] = extra.astype(BF16)


def scan_kernel(pay, after, out):
    blocks = pay.shape[0]
    state = jnp.zeros((2 * HEAD, 128), F32)
    out[blocks - 1] = state.astype(BF16)
    for k in range(blocks - 2, -1, -1):
        extra = pay[k + 1, 2 * HEAD :].astype(F32)
        one = jnp.broadcast_to(extra[0:1] + extra[1:2], (HEAD, 128))
        two = jnp.broadcast_to(extra[2:3] + extra[3:4], (HEAD, 128))
        through = jnp.concatenate([one, two], axis=0)
        state = through * state + pay[k + 1, : 2 * HEAD].astype(F32)
        out[k] = state.astype(BF16)


def conv_kernel(first, lengths, x, halo, step, taps, lagged, conv, upd, slope):
    heads = step.shape[1]
    rows = step.shape[2]
    start = first[0]
    low, _ = doc_bounds(start, lengths, rows)
    sub = iota((rows, rows), 0)
    lane = iota((rows, rows), 1)
    xt = jnp.transpose(x[0].astype(F32)).astype(BF16)
    lagged[0, 0] = xt
    hsub = iota((HALO, rows), 0)
    hlane = iota((HALO, rows), 1)
    for j in range(1, 4):
        here = ((sub + j == lane) & (sub + start >= low)).astype(BF16)
        away = ((hsub - HALO + j == hlane) & (hsub - HALO + start >= low)).astype(BF16)
        lagged[0, j] = (dot(xt, here) + dot(halo[0], away, TN)).astype(BF16)
    for h in range(heads):
        at = slice(h * HEAD, (h + 1) * HEAD)
        w = taps[0, at]
        pre = w[:, 4:5] + w[:, 0:1] * lagged[0, 0, at].astype(F32)
        for j in range(1, 4):
            pre = pre + w[:, j : j + 1] * lagged[0, j, at].astype(F32)
        sig = 1.0 / (1.0 + jnp.exp(-pre))
        co = (pre * sig).astype(BF16)
        conv[0, at] = co
        slope[0, at] = sig * (1.0 + pre * (1.0 - sig))
        upd[0, at] = (step[0, h : h + 1] * co.astype(F32)).astype(BF16)


def intra_kernel(
    first, lengths, skip, conv, upd, gy, gyt, bm, cm, step, rows_in, state, after,
    part, heads_out, gc, gb, acc, statec,
):
    g = pl.program_id(0)
    heads = step.shape[1]
    rows = step.shape[2]
    start = first[0]
    _, high = doc_bounds(start, lengths, rows)
    sub = iota((rows, rows), 0)
    lane = iota((rows, rows), 1)
    statec[...] = dot(state[0], cm[0], NT)
    gram = dot(cm[0], bm[0], NT)
    bias = jnp.where((sub >= lane) & (sub + start <= high), 0.0, -1e30)
    cum = rows_in[0, 0]
    cum_col = jnp.transpose(cum)
    acc[...] = jnp.zeros((rows, rows), F32)
    zero = jnp.zeros((HEAD, rows), BF16)
    spot = iota((heads, rows), 0)
    cum_out = jnp.zeros((heads, rows), F32)
    step_out = jnp.zeros((heads, rows), F32)
    skip_out = jnp.zeros((heads, rows), F32)
    for h in range(heads):
        at = slice(h * HEAD, (h + 1) * HEAD)
        co = conv[0, at].astype(F32)
        u = upd[0, at]
        st = step[0, h : h + 1]
        pair = gy[0, :, (h // 2) * 128 : (h // 2 + 1) * 128]
        both = jnp.concatenate([u, zero] if h % 2 == 0 else [zero, u], axis=0)
        score_grad = dot(pair, both)
        decay = jnp.exp2(cum_col[:, h : h + 1] - cum[h : h + 1] + bias)
        acc[...] += decay * score_grad
        score = (decay * gram).astype(BF16)
        gt = gyt[0, at]
        grad_u = dot(gt, score)
        y = dot(u, score, NT)
        gt = gt.astype(F32)
        row_sum = jnp.sum(gt * (y + rows_in[0, 1, h : h + 1] * statec[at]), axis=0, keepdims=True)
        col_sum = jnp.sum(u.astype(F32) * grad_u, axis=0, keepdims=True)
        cum_out = jnp.where(spot == h, row_sum - col_sum, cum_out)
        step_out = jnp.where(spot == h, jnp.sum(grad_u * co, axis=0, keepdims=True), step_out)
        skip_out = jnp.where(spot == h, jnp.sum(gt * co, axis=0, keepdims=True), skip_out)
        part[0, at] = st * grad_u + skip[g, h] * gt
    heads_out[0, 0] = cum_out
    heads_out[0, 1] = step_out
    heads_out[0, 2] = skip_out
    grad_gram = acc[...].astype(BF16)
    scaled = jnp.concatenate(
        [
            (gyt[0, h * HEAD : (h + 1) * HEAD].astype(F32) * rows_in[0, 1, h : h + 1]).astype(BF16)
            for h in range(heads)
        ],
        axis=0,
    )
    gc[0] = (dot(grad_gram, bm[0]) + dot(scaled, state[0], TN)).astype(BF16)
    gb[0] = dot(grad_gram, cm[0], TN)


def carry_kernel(
    rate, grad, bm, step, rows_in, heads_in, state, lagged, conv, slope, part,
    pay, grad_step, pre_out, edge, cols,
):
    g = pl.program_id(0)
    heads = step.shape[1]
    rows = step.shape[2]
    carry = dot(grad[0], bm[0], NT)
    spot = iota((heads, rows), 0)
    lane = iota((HEAD, 128), 1)
    to_end = rows_in[0, 2]
    along = jnp.zeros((heads, rows), F32)
    inner = jnp.zeros((heads, 128), F32)
    for h in range(heads):
        at = slice(h * HEAD, (h + 1) * HEAD)
        cb = carry[at]
        st = step[0, h : h + 1]
        along = jnp.where(spot == h, jnp.sum(cb * conv[0, at].astype(F32), axis=0, keepdims=True), along)
        prod = grad[0, at].astype(F32) * state[0, at].astype(F32)
        inner = jnp.where(
            iota((heads, 128), 0) == h, jnp.sum(prod, axis=0, keepdims=True), inner
        )
        gp = (part[0, at] + (st * to_end[h : h + 1]) * cb) * slope[0, at]
        pre_out[0, at] = gp.astype(BF16)
        out = jnp.where(lane == 12, jnp.sum(gp, axis=1, keepdims=True), gp[:, :128])
        for j in range(4):
            s = jnp.sum(gp * lagged[0, j, at].astype(F32), axis=1, keepdims=True)
            out = jnp.where(lane == 8 + j, s, out)
        cols[at] = out
    along = along * to_end
    step_two = along
    along = along * step[0]
    through = rows_in[0, 1][:, rows - 1 :]
    last = jnp.sum(along, axis=1, keepdims=True) + through * jnp.sum(inner, axis=1, keepdims=True)
    grad_cum = heads_in[0, 0] - along + jnp.where(iota((heads, rows), 1) == rows - 1, last, 0.0)
    back = (iota((rows, rows), 0) >= iota((rows, rows), 1)).astype(F32)
    grad_log = dot(grad_cum, back, precision=FULL)
    grad_step[0] = heads_in[0, 1] + step_two - per_head(rate, g, (heads, rows)) * grad_log
    lane = iota((heads, 128), 1)
    rate_grad = -jnp.sum(step[0] * grad_log, axis=1, keepdims=True)
    skip_grad = jnp.sum(heads_in[0, 2], axis=1, keepdims=True)
    top = cols[:heads]
    top = jnp.where(lane == 13, rate_grad, top)
    cols[:heads] = jnp.where(lane == 14, skip_grad, top)
    turned = jnp.transpose(cols[...])
    edge[0] = turned[:HALO].astype(BF16)
    pay[:, 0, 0] = jnp.broadcast_to(turned[8:16].astype(BF16), (pay.shape[0], 8, turned.shape[1]))


def grad_b_kernel(rows_in, upd, grad, gb, gc, edge, after, out, edge_out):
    edge_out[...] = edge[...]
    out[0, 1] = gc[0]
    heads = rows_in.shape[2]
    scaled = jnp.concatenate(
        [
            (upd[0, h * HEAD : (h + 1) * HEAD].astype(F32) * rows_in[0, 2, h : h + 1]).astype(BF16)
            for h in range(heads)
        ],
        axis=0,
    )
    out[0, 0] = (gb[0] + dot(scaled, grad[0], TN)).astype(BF16)


def input_kernel(first, lengths, pre, right, taps, out):
    rows = pre.shape[2]
    start = first[0]
    _, high = doc_bounds(start, lengths, rows)
    sub = iota((rows, rows), 0)
    lane = iota((rows, rows), 1)
    hsub = iota((HALO, rows), 0)
    hlane = iota((HALO, rows), 1)
    w = taps[0]
    total = w[:, 0:1] * pre[0].astype(F32)
    for j in range(1, 4):
        here = ((sub == lane + j) & (sub + start <= high)).astype(BF16)
        away = ((hsub + rows == hlane + j) & (hsub + rows + start <= high)).astype(BF16)
        total = total + w[:, j : j + 1] * (dot(pre[0], here) + dot(right[0], away, TN))
    out[0] = jnp.transpose(total).astype(BF16)


def spread_kernel(parts, out):
    total = parts[0].astype(F32)
    for i in range(1, parts.shape[0]):
        total = total + parts[i].astype(F32)
    out[...] = jnp.broadcast_to(total.astype(out.dtype), out.shape)


def final_kernel(core, mine, other, weight, bias, rate, skip):
    each = mine.shape[0]
    heads = rate.shape[1]
    for g in range(bias.shape[0]):
        ours = core[0] == g // each
        rows = jnp.where(ours, mine[g % each], other[g % each])
        for j in range(4):
            weight[j, g : g + 1] = rows[j : j + 1]
        bias[g : g + 1] = rows[4:5]
        rate[g : g + 1] = rows[5:6, :heads]
        skip[g : g + 1] = rows[6:7, :heads]


def pair_sum_kernel(parts, one, two):
    for out, i in ((one, 0), (two, 1)):
        total = parts[0, :, i].astype(F32)
        for p in range(1, parts.shape[0]):
            total = total + parts[p, :, i].astype(F32)
        out[...] = total


def sum_kernel(parts, out):
    total = parts[0].astype(F32)
    for i in range(1, parts.shape[0]):
        total = total + parts[i].astype(F32)
    out[...] = total.astype(out.dtype)


ANY = "any"


def call(kernel, grid, ins, outs, args, flops=0, nbytes=0, scratch=(), mib=60, specs=None):
    smem = pl.BlockSpec(memory_space=pltpu.SMEM)

    def spec(shape, blocked):
        if blocked is None:
            return smem
        if blocked is ANY:
            return pl.BlockSpec(memory_space=pl.ANY)
        if isinstance(blocked, pl.BlockSpec):
            return blocked
        if not blocked or not grid:
            return pl.BlockSpec(shape, lambda *i: (0,) * len(shape))
        return pl.BlockSpec(
            (shape[0] // grid[0],) + tuple(shape[1:]), lambda g: (g,) + (0,) * (len(shape) - 1)
        )

    return pl.pallas_call(
        kernel,
        grid=grid,
        in_specs=[spec(a.shape, b) for a, b in zip(args, ins)],
        out_specs=specs or [spec(s, True) for s, _ in outs],
        out_shape=[jax.ShapeDtypeStruct(s, t) for s, t in outs],
        scratch_shapes=list(scratch),
        cost_estimate=pl.CostEstimate(flops=flops, bytes_accessed=nbytes, transcendentals=0),
        compiler_params=pltpu.CompilerParams(vmem_limit_bytes=mib * 1024 * 1024),
    )(*args)


def shifted(block, axis, distance):
    size = lax.axis_size(axis)
    route = [(i, i + distance) for i in range(size) if 0 <= i + distance < size]
    return lax.ppermute(block, axis, route)


def body(
    conv_input,
    output_grad,
    b_matrix,
    c_matrix,
    step_size,
    decay_rate,
    skip_gain,
    conv_weight,
    conv_bias,
    saved_state,
    doc_lengths,
):
    _, rows, groups, features = conv_input.shape
    heads = step_size.shape[3]
    blocks = lax.axis_size("context")
    first = (lax.axis_index("context") * rows).astype(jnp.int32).reshape(1)
    x = jnp.transpose(conv_input[0], (1, 0, 2))
    gy = jnp.transpose(output_grad[0], (1, 0, 2))
    bm = jnp.transpose(b_matrix[0], (1, 0, 2))
    cm = jnp.transpose(c_matrix[0], (1, 0, 2))
    step = jnp.transpose(step_size[0], (1, 2, 0))
    state = saved_state.reshape(groups, features, 128)
    taps = jnp.concatenate(
        [
            jnp.transpose(conv_weight, (1, 2, 0)),
            conv_bias[:, :, None],
            jnp.zeros((groups, features, 3), F32),
        ],
        axis=2,
    )
    halo = shifted(conv_input[0, rows - HALO :], "context", 1)
    halo = jnp.transpose(halo, (1, 0, 2))

    wide = (groups, features, rows)
    pay, gyt, rows_in = call(
        offset_kernel,
        (groups,),
        [None, None, None, True, True, True],
        [
            ((groups * heads // 2, 2 * HEAD + EXTRA, 128), BF16),
            (wide, BF16),
            ((groups, 3, heads, rows), F32),
        ],
        (first, doc_lengths, decay_rate, step, gy, cm),
        flops=10**9,
        nbytes=4 * 10**6,
    )
    own = groups * heads // 2 // blocks
    gathered = lax.all_to_all(pay, "context", 0, 0, tiled=True)
    lagged, conv, upd, slope = call(
        conv_kernel,
        (groups,),
        [None, None] + [True] * 4,
        [
            ((groups, 4, features, rows), BF16),
            (wide, BF16),
            (wide, BF16),
            (wide, F32),
        ],
        (first, doc_lengths, x, halo, step, taps),
        flops=4 * 10**9,
        nbytes=10 * 10**6,
    )
    (scanned,) = call(
        scan_kernel,
        (),
        [True, ANY],
        [((blocks * own, 2 * HEAD, 128), BF16)],
        (gathered, upd),
        flops=10**7,
        nbytes=10**6,
    )
    part, heads_in, gc, gb = call(
        intra_kernel,
        (groups,),
        [None, None, None] + [True] * 9 + [ANY],
        [
            (wide, F32),
            ((groups, 3, heads, rows), F32),
            ((groups, rows, 128), BF16),
            ((groups, rows, 128), F32),
        ],
        (first, doc_lengths, skip_gain, conv, upd, gy, gyt, bm, cm, step, rows_in, state, scanned),
        flops=16 * 10**9,
        nbytes=10 * 10**6,
        scratch=(pltpu.VMEM((rows, rows), F32), pltpu.VMEM((features, rows), F32)),
    )
    grad = lax.all_to_all(scanned, "context", 0, 0, tiled=True).reshape(groups, features, 128)
    parts = lax.axis_size("tensor")
    here = groups // parts
    copies = lax.axis_size("dp")
    halves = 2 if copies % 2 == 0 else 1
    each = groups // halves
    wide_spec = pl.BlockSpec((1, features, rows), lambda g: (g, 0, 0))
    shares, grad_step, pre, edge = call(
        carry_kernel,
        (groups,),
        [None] + [True] * 10,
        [
            ((copies // halves, halves, each, 8, features), BF16),
            ((groups, heads, rows), F32),
            (wide, BF16),
            ((groups, HALO, features), BF16),
        ],
        (decay_rate, grad, bm, step, rows_in, heads_in, state, lagged, conv, slope, part),
        flops=10**9,
        nbytes=20 * 10**6,
        scratch=(pltpu.VMEM((features, 128), F32),),
        specs=[
            pl.BlockSpec(
                (copies // halves, 1, 1, 8, features), lambda g: (0, g // each, g % each, 0, 0)
            ),
            pl.BlockSpec((1, heads, rows), lambda g: (g, 0, 0)),
            wide_spec,
            pl.BlockSpec((1, HALO, features), lambda g: (g, 0, 0)),
        ],
    )
    small = (each, 8, features)
    shares = lax.all_to_all(shares.reshape((copies,) + small), "dp", 0, 0, tiled=True)
    (shares,) = call(spread_kernel, (), [True], [((blocks,) + small, BF16)], (shares,))
    gb, edge = call(
        grad_b_kernel,
        (groups,),
        [True] * 6 + [ANY],
        [((groups, 2, rows, 128), BF16), ((groups, HALO, features), BF16)],
        (rows_in, upd, grad, gb, gc, edge, shares),
        flops=10**8,
        nbytes=2 * 10**6,
    )
    shares = lax.all_to_all(shares, "context", 0, 0, tiled=True)
    (mine,) = call(sum_kernel, (), [True], [(small, F32)], (shares,))
    core = lax.axis_index("dp") % halves
    other = mine
    if halves == 2:
        other = lax.ppermute(mine, "dp", [(i, i ^ 1) for i in range(copies)])
    weight, bias, rate, skip = call(
        final_kernel,
        (),
        [None, True, True],
        [
            ((4, groups, features), F32),
            ((groups, features), F32),
            ((groups, heads), F32),
            ((groups, heads), F32),
        ],
        (core.astype(jnp.int32).reshape(1), mine, other),
    )
    both = lax.all_to_all(gb, "tensor", 0, 0, tiled=True).reshape(parts, here, 2, rows, 128)
    grad_b, grad_c = call(
        pair_sum_kernel, (), [True], [((here, rows, 128), F32)] * 2, (both,)
    )

    right = shifted(edge, "context", -1)
    (grad_input,) = call(
        input_kernel,
        (groups,),
        [None, None] + [True] * 3,
        [((groups, rows, features), BF16)],
        (first, doc_lengths, pre, right, taps),
        flops=10**9,
        nbytes=4 * 10**6,
    )
    return (
        jnp.transpose(grad_input, (1, 0, 2))[None],
        jnp.transpose(grad_b.reshape(1, here, rows, 128), (0, 2, 1, 3)),
        jnp.transpose(grad_c.reshape(1, here, rows, 128), (0, 2, 1, 3)),
        jnp.transpose(grad_step, (2, 0, 1))[None],
        weight,
        bias,
        rate,
        skip,
    )


def solution(mesh):
    return jax.shard_map(
        body,
        mesh=mesh,
        in_specs=(
            P("dp", "context", None, "tensor"),
            P("dp", "context", None, "tensor"),
            P("dp", "context", None, None),
            P("dp", "context", None, None),
            P("dp", "context", None, "tensor"),
            P(None, "tensor"),
            P(None, "tensor"),
            P(None, None, "tensor"),
            P(None, "tensor"),
            P("dp", "context", None, "tensor", None, None),
            P("dp", None),
        ),
        out_specs=(
            P("dp", "context", None, "tensor"),
            P("dp", "context", "tensor", None),
            P("dp", "context", "tensor", None),
            P("dp", "context", None, "tensor"),
            P(None, None, "tensor"),
            P(None, "tensor"),
            P(None, "tensor"),
            P(None, "tensor"),
        ),
        check_vma=False,
    )
```

```python
import functools

import jax
import jax.numpy as jnp
from jax import lax
from jax.experimental import pallas as pl
from jax.experimental.pallas import tpu as pltpu
from jax.sharding import PartitionSpec as P

F32 = jnp.float32
BF16 = jnp.bfloat16
LOG2E = 1.4426950408889634
FULL = lax.Precision.HIGHEST
HEAD = 64
HALO = 8
EXTRA = 16
ROWS = 24
FAR = 1 << 28


def dot(a, b, dims=((1,), (0,)), precision=None):
    return lax.dot_general(a, b, (dims, ((), ())), precision=precision, preferred_element_type=F32)


NT = ((1,), (1,))
TN = ((0,), (0,))


def iota(shape, axis):
    return lax.broadcasted_iota(jnp.int32, shape, axis)


def doc_bounds(first, lengths, rows):
    pos = first + iota((1, rows), 1)
    low = jnp.zeros((1, rows), jnp.int32)
    high = jnp.full((1, rows), FAR, jnp.int32)
    start = jnp.int32(0)
    for d in range(lengths.shape[1]):
        low = jnp.where(pos >= start, start, low)
        start = start + lengths[0, d]
        high = jnp.minimum(high, jnp.where(start > pos, start - 1, FAR))
    return low, high


def per_head(values, group, shape):
    column = jnp.zeros(shape, F32)
    for h in range(shape[0]):
        column = jnp.where(iota(shape, 0) == h, values[group, h], column)
    return column


def summed(values, chosen):
    count = values.shape[0]
    upper = values.astype(BF16).astype(F32)
    rest = values - upper
    middle = rest.astype(BF16).astype(F32)
    parts = jnp.concatenate([upper, middle, rest - middle], axis=0).astype(BF16)
    out = dot(parts, chosen)
    return out[:count] + out[count : 2 * count] + out[2 * count :]


def offset_kernel(first, lengths, rate, step, gy, cm, pay, gyt, rows_out, tri):
    g = pl.program_id(0)

    @pl.when(g == 0)
    def _():
        size = tri.shape
        tri[...] = (iota(size, 0) <= iota(size, 1)).astype(BF16)

    rows = step.shape[2]
    heads = step.shape[1]
    low, high = doc_bounds(first[0], lengths, rows)
    cum = summed(step[0] * (per_head(rate, g, (heads, rows)) * (-LOG2E)), tri[...])
    from_start = jnp.where(low < first[0], jnp.exp2(cum), 0.0)
    last = jnp.broadcast_to(cum[:, rows - 1 :], (heads, rows))
    to_end = jnp.where(high >= first[0] + rows - 1, jnp.exp2(jnp.minimum(last - cum, 0.0)), 0.0)
    rows_out[0, 0] = cum
    rows_out[0, 1] = from_start
    rows_out[0, 2] = to_end
    gt = jnp.transpose(gy[0].astype(F32))
    gyt[0] = gt.astype(BF16)
    scaled = jnp.concatenate(
        [gt[h * HEAD : (h + 1) * HEAD] * from_start[h : h + 1] for h in range(heads)], axis=0
    ).astype(BF16)
    pay[0, : heads * HEAD] = dot(scaled, cm[0]).astype(BF16)
    pay[0, heads * HEAD :] = factors_out(jnp.broadcast_to(from_start[:, rows - 1 :], (heads, 128)))


def factors_out(values):
    upper = values.astype(BF16).astype(F32)
    return jnp.concatenate([upper, values - upper], axis=0).astype(BF16)


def factors_in(rows):
    rows = rows.astype(F32)
    half = rows.shape[0] // 2
    return rows[:half] + rows[half:]


def quad_kernel(got, out):
    count = got.shape[0]
    size = got.shape[1] - EXTRA
    through = [factors_in(got[r, size:]) for r in range(count)]
    total = through[0]
    for r in range(1, count):
        total = total * through[r]
    for h in range(size // HEAD):
        at = slice(h * HEAD, (h + 1) * HEAD)
        state = got[count - 1, at].astype(F32)
        for r in range(count - 2, -1, -1):
            state = through[r][h : h + 1] * state + got[r, at].astype(F32)
        out[at] = state.astype(BF16)
    out[size:] = factors_out(total)


def scan_kernel(got, near, far, after, out):
    count = got.shape[0]
    size = got.shape[1] - EXTRA
    through = [factors_in(got[r, size:]) for r in range(count)]
    total = factors_in(near[size:])
    for h in range(size // HEAD):
        at = slice(h * HEAD, (h + 1) * HEAD)
        state = near[at].astype(F32) + total[h : h + 1] * far[at].astype(F32)
        out[count - 1, at] = state.astype(BF16)
        for r in range(count - 2, -1, -1):
            state = through[r + 1][h : h + 1] * state + got[r + 1, at].astype(F32)
            out[r, at] = state.astype(BF16)


def conv_kernel(first, lengths, x, halo, step, taps, after, lagged, conv, upd, slope):
    heads = step.shape[1]
    rows = step.shape[2]
    start = first[0]
    low, _ = doc_bounds(start, lengths, rows)
    sub = iota((rows, rows), 0)
    lane = iota((rows, rows), 1)
    xt = jnp.transpose(x[0].astype(F32)).astype(BF16)
    lagged[0, 0] = xt
    hsub = iota((HALO, rows), 0)
    hlane = iota((HALO, rows), 1)
    for j in range(1, 4):
        here = ((sub + j == lane) & (sub + start >= low)).astype(BF16)
        away = ((hsub - HALO + j == hlane) & (hsub - HALO + start >= low)).astype(BF16)
        lagged[0, j] = (dot(xt, here) + dot(halo[0], away, TN)).astype(BF16)
    for h in range(heads):
        at = slice(h * HEAD, (h + 1) * HEAD)
        w = taps[0, at]
        pre = w[:, 4:5] + w[:, 0:1] * lagged[0, 0, at].astype(F32)
        for j in range(1, 4):
            pre = pre + w[:, j : j + 1] * lagged[0, j, at].astype(F32)
        sig = 1.0 / (1.0 + jnp.exp(-pre))
        co = (pre * sig).astype(BF16)
        conv[0, at] = co
        slope[0, at] = (sig * (1.0 + pre * (1.0 - sig))).astype(BF16)
        upd[0, at] = (step[0, h : h + 1] * co.astype(F32)).astype(BF16)


def intra_kernel(
    first, lengths, skip, conv, upd, gy, gyt, bm, cm, step, rows_in, state, after,
    part, heads_out, gc, gb, acc, statec,
):
    g = pl.program_id(0)
    heads = step.shape[1]
    rows = step.shape[2]
    start = first[0]
    _, high = doc_bounds(start, lengths, rows)
    sub = iota((rows, rows), 0)
    lane = iota((rows, rows), 1)
    statec[...] = dot(state[0], cm[0], NT)
    gram = dot(cm[0], bm[0], NT)
    bias = jnp.where((sub >= lane) & (sub + start <= high), 0.0, -1e30)
    cum = rows_in[0, 0]
    cum_col = jnp.transpose(cum)
    acc[...] = jnp.zeros((rows, rows), F32)
    zero = jnp.zeros((HEAD, rows), BF16)
    spot = iota((heads, rows), 0)
    cum_out = jnp.zeros((heads, rows), F32)
    step_out = jnp.zeros((heads, rows), F32)
    skip_out = jnp.zeros((heads, rows), F32)
    for h in range(heads):
        at = slice(h * HEAD, (h + 1) * HEAD)
        co = conv[0, at].astype(F32)
        u = upd[0, at]
        st = step[0, h : h + 1]
        pair = gy[0, :, (h // 2) * 128 : (h // 2 + 1) * 128]
        both = jnp.concatenate([u, zero] if h % 2 == 0 else [zero, u], axis=0)
        score_grad = dot(pair, both)
        decay = jnp.exp2(cum_col[:, h : h + 1] - cum[h : h + 1] + bias)
        acc[...] += decay * score_grad
        score = (decay * gram).astype(BF16)
        gt = gyt[0, at]
        grad_u = dot(gt, score)
        y = dot(u, score, NT)
        gt = gt.astype(F32)
        row_sum = jnp.sum(gt * (y + rows_in[0, 1, h : h + 1] * statec[at]), axis=0, keepdims=True)
        col_sum = jnp.sum(u.astype(F32) * grad_u, axis=0, keepdims=True)
        cum_out = jnp.where(spot == h, row_sum - col_sum, cum_out)
        step_out = jnp.where(spot == h, jnp.sum(grad_u * co, axis=0, keepdims=True), step_out)
        skip_out = jnp.where(spot == h, jnp.sum(gt * co, axis=0, keepdims=True), skip_out)
        part[0, at] = (st * grad_u + skip[g, h] * gt).astype(BF16)
    heads_out[0, 0] = cum_out
    heads_out[0, 1] = step_out
    heads_out[0, 2] = skip_out
    grad_gram = acc[...].astype(BF16)
    scaled = jnp.concatenate(
        [
            (gyt[0, h * HEAD : (h + 1) * HEAD].astype(F32) * rows_in[0, 1, h : h + 1]).astype(BF16)
            for h in range(heads)
        ],
        axis=0,
    )
    gc[0] = (dot(grad_gram, bm[0]) + dot(scaled, state[0], TN)).astype(BF16)
    gb[0] = dot(grad_gram, cm[0], TN)


def carry_kernel(
    rate, grad, bm, step, rows_in, heads_in, state, lagged, conv, slope, part,
    after, pay, grad_step, pre_out, edge, prods, tri,
):
    group = pl.program_id(0)

    @pl.when(group == 0)
    def _():
        size = tri.shape
        tri[...] = (iota(size, 0) >= iota(size, 1)).astype(BF16)

    heads = step.shape[1]
    rows = step.shape[2]
    carry = dot(grad[0], bm[0], NT)
    spot = iota((heads, rows), 0)
    to_end = rows_in[0, 2]
    along = jnp.zeros((heads, rows), F32)
    inner = jnp.zeros((heads, 128), F32)
    for h in range(heads):
        at = slice(h * HEAD, (h + 1) * HEAD)
        cb = carry[at]
        st = step[0, h : h + 1]
        along = jnp.where(spot == h, jnp.sum(cb * conv[0, at].astype(F32), axis=0, keepdims=True), along)
        prod = grad[0, at].astype(F32) * state[0, at].astype(F32)
        inner = jnp.where(
            iota((heads, 128), 0) == h, jnp.sum(prod, axis=0, keepdims=True), inner
        )
        gp = part[0, at].astype(F32) + (st * to_end[h : h + 1]) * cb
        gp = gp * slope[0, at].astype(F32)
        pre_out[0, at] = gp.astype(BF16)
        terms = [gp * lagged[0, j, at].astype(F32) for j in range(4)] + [gp]
        for j, term in enumerate(terms):
            lanes = slice(j % 2 * 128, j % 2 * 128 + 128)
            prods[j // 2, at, lanes] = (term[:, :128] + term[:, 128:]).astype(BF16)
        prods[2, at, 128:] = gp[:, :128].astype(BF16)
    along = along * to_end
    step_two = along
    along = along * step[0]
    through = rows_in[0, 1][:, rows - 1 :]
    last = jnp.sum(along, axis=1, keepdims=True) + through * jnp.sum(inner, axis=1, keepdims=True)
    grad_cum = heads_in[0, 0] - along + jnp.where(iota((heads, rows), 1) == rows - 1, last, 0.0)
    grad_log = summed(grad_cum, tri[...])
    grad_step[0] = heads_in[0, 1] + step_two - per_head(rate, group, (heads, rows)) * grad_log
    spot = iota((ROWS + HALO, rows), 0)
    lane = iota((ROWS + HALO, rows), 1)
    total = jnp.zeros((ROWS, 128), F32)
    for i in range(prods.shape[1] // 128):
        at = slice(i * 128, (i + 1) * 128)
        for k in range(3):
            if k < 2:
                chosen = spot == i * 5 + 2 * k + (lane >= 128).astype(jnp.int32)
            else:
                chosen = spot == jnp.where(lane < 128, i * 5 + 4, ROWS + lane - 128)
            out = dot(chosen.astype(BF16), prods[k, at], NT)
            total = total + out[:ROWS]
        edge[0, :, at] = out[ROWS:].astype(BF16)
    few = jnp.concatenate([-step[0] * grad_log, heads_in[0, 2]], axis=0)
    upper = few.astype(BF16).astype(F32)
    few = jnp.concatenate([upper, few - upper], axis=1)
    few = jnp.concatenate([few, jnp.zeros((128 - 2 * heads, 2 * rows), F32)], axis=0).astype(BF16)
    total = total + dot((iota((ROWS, 2 * rows), 0) == 20).astype(BF16), few, NT)
    pay[:, 0, 0] = jnp.broadcast_to(total.astype(BF16), (pay.shape[0], ROWS, 128))


def grad_b_kernel(index, rows_in, upd, grad, gb, gc, after, *outs):
    heads = rows_in.shape[2]
    scaled = jnp.concatenate(
        [
            (upd[0, h * HEAD : (h + 1) * HEAD].astype(F32) * rows_in[0, 2, h : h + 1]).astype(BF16)
            for h in range(heads)
        ],
        axis=0,
    )
    total = (gb[0] + dot(scaled, grad[0], TN)).astype(BF16)
    for r, out in enumerate(outs):

        @pl.when(pl.program_id(0) == r)
        def _():
            out[0] = total
            out[1] = gc[0]


def input_kernel(first, lengths, pre, right, taps, out, here, away):
    rows = pre.shape[2]

    @pl.when(pl.program_id(0) == 0)
    def _():
        start = first[0]
        _, high = doc_bounds(start, lengths, rows)
        for j in range(1, 4):
            sub = iota((rows, rows), 0)
            lane = iota((rows, rows), 1)
            here[j - 1] = ((sub == lane + j) & (sub + start <= high)).astype(BF16)
            sub = iota((HALO, rows), 0) + rows
            lane = iota((HALO, rows), 1)
            away[j - 1] = ((sub == lane + j) & (sub + start <= high)).astype(F32)

    w = taps[0]
    total = w[:, 0:1] * pre[0].astype(F32)
    for j in range(1, 4):
        far = dot(right[0], away[j - 1].astype(BF16), TN)
        total = total + w[:, j : j + 1] * (dot(pre[0], here[j - 1]) + far)
    out[0] = jnp.transpose(total).astype(BF16)


def spread_kernel(parts, *refs, groups):
    out = refs[groups + 1]
    total = parts[0].astype(F32)
    for i in range(1, parts.shape[0]):
        total = total + parts[i].astype(F32)
    out[...] = jnp.broadcast_to(total.astype(out.dtype), out.shape)


def final_kernel(core, mine, other, weight, bias, rate, skip):
    each = mine.shape[0]
    heads = rate.shape[1]
    for g in range(bias.shape[0]):
        ours = core[0] == g // each
        rows = jnp.where(ours, mine[g % each], other[g % each])
        for i in range(bias.shape[1] // 128):
            at = slice(i * 128, (i + 1) * 128)
            for j in range(4):
                weight[j, g : g + 1, at] = rows[i * 5 + j : i * 5 + j + 1]
            bias[g : g + 1, at] = rows[i * 5 + 4 : i * 5 + 5]
        rate[g : g + 1] = rows[20:21, :heads]
        skip[g : g + 1] = rows[20:21, heads : 2 * heads]


def pair_sum_kernel(*refs):
    parts, outs = refs[:-2], refs[-2:]
    for i, out in enumerate(outs):
        total = parts[0][i].astype(F32)
        for part in parts[1:]:
            total = total + part[i].astype(F32)
        out[...] = total


def sum_kernel(parts, *refs):
    out = refs[-1]
    total = parts[0].astype(F32)
    for i in range(1, parts.shape[0]):
        total = total + parts[i].astype(F32)
    out[...] = total.astype(out.dtype)


ANY = pl.BlockSpec(memory_space=pl.ANY)
SMEM = pl.BlockSpec(memory_space=pltpu.SMEM)


def whole(shape):
    return pl.BlockSpec(shape, lambda *i: (0,) * len(shape))


def by_group(array, at=0):
    tail = tuple(array.shape[1:])
    return pl.BlockSpec((1,) + tail, lambda g: (g + at,) + (0,) * len(tail))


def array(shape, dtype):
    return jax.ShapeDtypeStruct(shape, dtype)


def call(kernel, grid, ins, outs, flops=0, nbytes=0, scratch=(), alias=None, mib=24):
    return pl.pallas_call(
        kernel,
        grid=grid,
        in_specs=[s for s, _ in ins],
        out_specs=[s for s, _ in outs],
        out_shape=[o for _, o in outs],
        scratch_shapes=list(scratch),
        input_output_aliases=alias or {},
        cost_estimate=pl.CostEstimate(flops=flops, bytes_accessed=nbytes, transcendentals=0),
        compiler_params=pltpu.CompilerParams(vmem_limit_bytes=mib * 1024 * 1024),
    )(*[a for _, a in ins])


def shifted(block, axis, distance):
    size = lax.axis_size(axis)
    route = [(i, i + distance) for i in range(size) if 0 <= i + distance < size]
    return lax.ppermute(block, axis, route)


def body(
    conv_input,
    output_grad,
    b_matrix,
    c_matrix,
    step_size,
    decay_rate,
    skip_gain,
    conv_weight,
    conv_bias,
    saved_state,
    doc_lengths,
):
    _, rows, groups, features = conv_input.shape
    heads = step_size.shape[3]
    blocks = lax.axis_size("context")
    first = (lax.axis_index("context") * rows).astype(jnp.int32).reshape(1)
    x = jnp.transpose(conv_input[0], (1, 0, 2))
    gy = jnp.transpose(output_grad[0], (1, 0, 2))
    bm = jnp.transpose(b_matrix[0], (1, 0, 2))
    cm = jnp.transpose(c_matrix[0], (1, 0, 2))
    step = jnp.transpose(step_size[0], (1, 2, 0))
    state = saved_state.reshape(groups, features, 128)
    taps = jnp.concatenate(
        [
            jnp.transpose(conv_weight, (1, 2, 0)),
            conv_bias[:, :, None],
            jnp.zeros((groups, features, 3), F32),
        ],
        axis=2,
    )
    sent = shifted(conv_input[0, rows - HALO :], "context", 1)
    halo = jnp.transpose(sent, (1, 0, 2))

    wide = array((groups, features, rows), BF16)
    per_row = array((groups, 3, heads, rows), F32)
    quads = [[q * groups + r for r in range(groups)] for q in range(blocks // groups)]
    size = features + EXTRA
    pay = array((groups, size, 128), BF16)
    pay, gyt, rows_in = call(
        offset_kernel,
        (groups,),
        [(SMEM, a) for a in (first, doc_lengths, decay_rate)]
        + [(by_group(a), a) for a in (step, gy, cm)],
        [(by_group(a), a) for a in (pay, wide, per_row)],
        flops=10**9,
        nbytes=4 * 10**6,
        mib=60,
        scratch=(pltpu.VMEM((rows, rows), BF16),),
    )

    def across(block, axis, among=None):
        return lax.all_to_all(block, axis, 0, 0, axis_index_groups=among, tiled=True)

    got = across(pay, "context", quads)
    quad = array((size, 128), BF16)
    (quad,) = call(
        quad_kernel,
        (),
        [(whole(got.shape), got)],
        [(whole(quad.shape), quad)],
        flops=10**7,
        nbytes=10**6,
    )
    near = shifted(quad, "context", -groups)
    far = shifted(quad, "context", -2 * groups)
    lags = array((groups, 4, features, rows), BF16)
    lagged, conv, upd, slope = call(
        conv_kernel,
        (groups,),
        [(SMEM, first), (SMEM, doc_lengths)]
        + [(by_group(a), a) for a in (x, halo, step, taps)]
        + [(ANY, quad)],
        [(by_group(a), a) for a in (lags, wide, wide, wide)],
        flops=4 * 10**9,
        nbytes=10 * 10**6,
        mib=60,
    )
    states = array((groups, features, 128), BF16)
    (states,) = call(
        scan_kernel,
        (),
        [(whole(a.shape), a) for a in (got, near, far)] + [(ANY, upd)],
        [(whole(states.shape), states)],
        flops=10**7,
        nbytes=10**6,
    )
    gram_out = array((groups, rows, 128), BF16)
    gram_out32 = array((groups, rows, 128), F32)
    part, heads_in, gc, gb = call(
        intra_kernel,
        (groups,),
        [(SMEM, first), (SMEM, doc_lengths), (SMEM, skip_gain)]
        + [(by_group(a), a) for a in (conv, upd, gy, gyt, bm, cm, step, rows_in, state)]
        + [(ANY, states)],
        [(by_group(a), a) for a in (wide, per_row, gram_out, gram_out32)],
        flops=16 * 10**9,
        nbytes=10 * 10**6,
        mib=60,
        scratch=(pltpu.VMEM((rows, rows), F32), pltpu.VMEM((features, rows), F32)),
    )
    grad = across(states, "context", quads)

    copies = lax.axis_size("dp")
    halves = 2 if copies % 2 == 0 else 1
    each = groups // halves
    parts = lax.axis_size("tensor")
    shares = array((copies // halves, halves, each, ROWS, 128), BF16)
    step_out = array((groups, heads, rows), F32)
    edges = array((groups, HALO, features), BF16)
    shared, grad_step, pre, edge = call(
        carry_kernel,
        (groups,),
        [(SMEM, decay_rate)]
        + [
            (by_group(a), a)
            for a in (grad, bm, step, rows_in, heads_in, state, lagged, conv, slope, part)
        ]
        + [(ANY, gc)],
        [
            (
                pl.BlockSpec(
                    (copies // halves, 1, 1, ROWS, 128),
                    lambda g: (0, g // each, g % each, 0, 0),
                ),
                shares,
            ),
        ]
        + [(by_group(a), a) for a in (step_out, wide, edges)],
        flops=10**9,
        nbytes=8 * 10**6,
        mib=60,
        scratch=(pltpu.VMEM((3, features, rows), BF16), pltpu.VMEM((rows, rows), BF16)),
    )
    assert parts in (1, groups)
    index = lax.axis_index("tensor").astype(jnp.int32).reshape(1)

    def turned(a):
        tail = tuple(a.shape[1:])
        return pl.BlockSpec(
            (1,) + tail, lambda r, i: ((i[0] + r) % groups,) + (0,) * len(tail)
        )

    pair = (2, rows, 128)
    held = pl.pallas_call(
        grad_b_kernel,
        grid_spec=pltpu.PrefetchScalarGridSpec(
            num_scalar_prefetch=1,
            grid=(groups,),
            in_specs=[turned(a) for a in (rows_in, upd, grad, gb, gc)] + [ANY],
            out_specs=[pl.BlockSpec(pair, lambda r, i: (0, 0, 0))] * groups,
        ),
        out_shape=[array(pair, BF16)] * groups,
        cost_estimate=pl.CostEstimate(flops=10**8, bytes_accessed=2 * 10**6, transcendentals=0),
        compiler_params=pltpu.CompilerParams(vmem_limit_bytes=24 * 1024 * 1024),
    )(index, rows_in, upd, grad, gb, gc, shared)

    small = (each, ROWS, 128)
    shared = across(shared.reshape((copies,) + small), "dp")
    spread = array((blocks,) + small, BF16)
    right = shifted(edge, "context", -1)
    shared, *held = call(
        functools.partial(spread_kernel, groups=groups),
        (),
        [(whole(shared.shape), shared)] + [(ANY, h) for h in held] + [(ANY, right)],
        [(whole(spread.shape), spread)] + [(ANY, array(pair, BF16))] * groups,
        alias={1 + i: 1 + i for i in range(groups)},
    )
    shared = across(shared, "context")
    part_out = array((rows, 128), F32)

    def pair_sum(held):
        return call(
            pair_sum_kernel,
            (),
            [(whole(pair), h) for h in held],
            [(whole(part_out.shape), part_out)] * 2,
        )

    if parts == groups:
        held = [
            lax.ppermute(h, "tensor", [(i, (i + r) % parts) for i in range(parts)]) if r else h
            for r, h in enumerate(held)
        ]
        grad_b, grad_c = [p[None] for p in pair_sum(held)]
    else:
        grad_b, grad_c = [jnp.stack(p) for p in zip(*[pair_sum([h]) for h in held])]
    natural = array((groups, rows, features), BF16)
    (grad_input,) = call(
        input_kernel,
        (groups,),
        [(SMEM, first), (SMEM, doc_lengths)] + [(by_group(a), a) for a in (pre, right, taps)],
        [(by_group(natural), natural)],
        flops=10**9,
        nbytes=4 * 10**6,
        mib=60,
        scratch=(pltpu.VMEM((3, rows, rows), BF16), pltpu.VMEM((3, HALO, rows), F32)),
    )
    (mine,) = call(
        sum_kernel,
        (),
        [(whole(shared.shape), shared), (ANY, grad_input)],
        [(whole(small), array(small, F32))],
    )
    core = lax.axis_index("dp") % halves
    other = mine
    if halves == 2:
        other = lax.ppermute(mine, "dp", [(i, i ^ 1) for i in range(copies)])
    outs = [(4, groups, features), (groups, features), (groups, heads), (groups, heads)]
    weight, bias, rate, skip = call(
        final_kernel,
        (),
        [(SMEM, core.astype(jnp.int32).reshape(1)), (whole(small), mine), (whole(small), other)],
        [(whole(o), array(o, F32)) for o in outs],
    )
    return (
        jnp.transpose(grad_input, (1, 0, 2))[None],
        jnp.transpose(grad_b[None], (0, 2, 1, 3)),
        jnp.transpose(grad_c[None], (0, 2, 1, 3)),
        jnp.transpose(grad_step, (2, 0, 1))[None],
        weight,
        bias,
        rate,
        skip,
    )


def solution(mesh):
    return jax.shard_map(
        body,
        mesh=mesh,
        in_specs=(
            P("dp", "context", None, "tensor"),
            P("dp", "context", None, "tensor"),
            P("dp", "context", None, None),
            P("dp", "context", None, None),
            P("dp", "context", None, "tensor"),
            P(None, "tensor"),
            P(None, "tensor"),
            P(None, None, "tensor"),
            P(None, "tensor"),
            P("dp", "context", None, "tensor", None, None),
            P("dp", None),
        ),
        out_specs=(
            P("dp", "context", None, "tensor"),
            P("dp", "context", "tensor", None),
            P("dp", "context", "tensor", None),
            P("dp", "context", None, "tensor"),
            P(None, None, "tensor"),
            P(None, "tensor"),
            P(None, "tensor"),
            P(None, "tensor"),
        ),
        check_vma=False,
    )
```

```python
import functools

import jax
import jax.numpy as jnp
from jax import lax
from jax.experimental import pallas as pl
from jax.experimental.pallas import tpu as pltpu
from jax.sharding import PartitionSpec as P

F32 = jnp.float32
BF16 = jnp.bfloat16
LOG2E = 1.4426950408889634
FULL = lax.Precision.HIGHEST
HEAD = 64
HALO = 8
EXTRA = 16
ROWS = 24
FAR = 1 << 28


def dot(a, b, dims=((1,), (0,)), precision=None):
    return lax.dot_general(a, b, (dims, ((), ())), precision=precision, preferred_element_type=F32)


NT = ((1,), (1,))
TN = ((0,), (0,))


def iota(shape, axis):
    return lax.broadcasted_iota(jnp.int32, shape, axis)


def doc_bounds(first, lengths, rows):
    pos = first + iota((1, rows), 1)
    low = jnp.zeros((1, rows), jnp.int32)
    high = jnp.full((1, rows), FAR, jnp.int32)
    start = jnp.int32(0)
    for d in range(lengths.shape[1]):
        low = jnp.where(pos >= start, start, low)
        start = start + lengths[0, d]
        high = jnp.minimum(high, jnp.where(start > pos, start - 1, FAR))
    return low, high


def per_head(values, group, shape):
    column = jnp.zeros(shape, F32)
    for h in range(shape[0]):
        column = jnp.where(iota(shape, 0) == h, values[group, h], column)
    return column


def summed(values, chosen):
    count = values.shape[0]
    upper = values.astype(BF16).astype(F32)
    rest = values - upper
    middle = rest.astype(BF16).astype(F32)
    parts = jnp.concatenate([upper, middle, rest - middle], axis=0).astype(BF16)
    out = dot(parts, chosen)
    return out[:count] + out[count : 2 * count] + out[2 * count :]


def offset_kernel(shift, first, lengths, rate, step, gy, cm, pay, gyt, rows_out, tri):
    g = pl.program_id(0)

    @pl.when(g == 0)
    def _():
        size = tri.shape
        tri[...] = (iota(size, 0) <= iota(size, 1)).astype(BF16)

    rows = step.shape[2]
    heads = step.shape[1]
    low, high = doc_bounds(first[0], lengths, rows)
    cum = summed(step[0] * (per_head(rate, g, (heads, rows)) * (-LOG2E)), tri[...])
    from_start = jnp.where(low < first[0], jnp.exp2(cum), 0.0)
    last = jnp.broadcast_to(cum[:, rows - 1 :], (heads, rows))
    to_end = jnp.where(high >= first[0] + rows - 1, jnp.exp2(jnp.minimum(last - cum, 0.0)), 0.0)
    rows_out[0, 0] = cum
    rows_out[0, 1] = from_start
    rows_out[0, 2] = to_end
    gt = jnp.transpose(gy[0].astype(F32))
    gyt[0] = gt.astype(BF16)
    scaled = jnp.concatenate(
        [gt[h * HEAD : (h + 1) * HEAD] * from_start[h : h + 1] for h in range(heads)], axis=0
    ).astype(BF16)
    pay[0, : heads * HEAD] = dot(scaled, cm[0]).astype(BF16)
    pay[0, heads * HEAD :] = factors_out(jnp.broadcast_to(from_start[:, rows - 1 :], (heads, 128)))


def factors_out(values):
    upper = values.astype(BF16).astype(F32)
    return jnp.concatenate([upper, values - upper], axis=0).astype(BF16)


def factors_in(rows):
    rows = rows.astype(F32)
    half = rows.shape[0] // 2
    return rows[:half] + rows[half:]


def quad_kernel(got, out):
    count = got.shape[0]
    size = got.shape[1] - EXTRA
    through = [factors_in(got[r, size:]) for r in range(count)]
    total = through[0]
    for r in range(1, count):
        total = total * through[r]
    for h in range(size // HEAD):
        at = slice(h * HEAD, (h + 1) * HEAD)
        state = got[count - 1, at].astype(F32)
        for r in range(count - 2, -1, -1):
            state = through[r][h : h + 1] * state + got[r, at].astype(F32)
        out[at] = state.astype(BF16)
    out[size:] = factors_out(total)


def scan_kernel(got, near, far, after, out):
    count = got.shape[0]
    size = got.shape[1] - EXTRA
    through = [factors_in(got[r, size:]) for r in range(count)]
    total = factors_in(near[size:])
    for h in range(size // HEAD):
        at = slice(h * HEAD, (h + 1) * HEAD)
        state = near[at].astype(F32) + total[h : h + 1] * far[at].astype(F32)
        out[count - 1, at] = state.astype(BF16)
        for r in range(count - 2, -1, -1):
            state = through[r + 1][h : h + 1] * state + got[r + 1, at].astype(F32)
            out[r, at] = state.astype(BF16)


def lag_masks(first, lengths, here, away):
    rows = here.shape[2]
    start = first[0]
    low, _ = doc_bounds(start, lengths, rows)
    for j in range(1, 4):
        sub = iota((rows, rows), 0)
        lane = iota((rows, rows), 1)
        here[j - 1] = ((sub + j == lane) & (sub + start >= low)).astype(BF16)
        sub = iota((HALO, rows), 0) - HALO
        lane = iota((HALO, rows), 1)
        away[j - 1] = ((sub + j == lane) & (sub + start >= low)).astype(F32)


def lag(xt, halo, here, away, j):
    return dot(xt, here[j - 1]) + dot(halo, away[j - 1].astype(BF16), TN)


def conv_kernel(
    first, lengths, x, halo, step, taps, after, lagged, conv, upd, slope, here, away
):
    heads = step.shape[1]

    @pl.when(pl.program_id(0) == 0)
    def _():
        lag_masks(first, lengths, here, away)

    xt = jnp.transpose(x[0].astype(F32)).astype(BF16)
    lagged[0, 0] = xt
    for j in range(1, 4):
        lagged[0, j] = lag(xt, halo[0], here, away, j).astype(BF16)
    for h in range(heads):
        at = slice(h * HEAD, (h + 1) * HEAD)
        w = taps[0, at]
        pre = w[:, 4:5] + w[:, 0:1] * lagged[0, 0, at].astype(F32)
        for j in range(1, 4):
            pre = pre + w[:, j : j + 1] * lagged[0, j, at].astype(F32)
        sig = 1.0 / (1.0 + jnp.exp(-pre))
        co = (pre * sig).astype(BF16)
        conv[0, at] = co
        slope[0, at] = (sig * (1.0 + pre * (1.0 - sig))).astype(BF16)
        upd[0, at] = (step[0, h : h + 1] * co.astype(F32)).astype(BF16)


def intra_kernel(
    first, lengths, skip, conv, upd, gy, gyt, bm, cm, step, rows_in, state, after,
    part, heads_out, gc, gb, acc, statec,
):
    g = pl.program_id(0)
    heads = step.shape[1]
    rows = step.shape[2]
    start = first[0]
    _, high = doc_bounds(start, lengths, rows)
    sub = iota((rows, rows), 0)
    lane = iota((rows, rows), 1)
    statec[...] = dot(state[0], cm[0], NT)
    gram = dot(cm[0], bm[0], NT)
    bias = jnp.where((sub >= lane) & (sub + start <= high), 0.0, -1e30)
    cum = rows_in[0, 0]
    cum_col = jnp.transpose(cum)
    acc[...] = jnp.zeros((rows, rows), F32)
    zero = jnp.zeros((HEAD, rows), BF16)
    spot = iota((heads, rows), 0)
    cum_out = jnp.zeros((heads, rows), F32)
    step_out = jnp.zeros((heads, rows), F32)
    skip_out = jnp.zeros((heads, rows), F32)
    for h in range(heads):
        at = slice(h * HEAD, (h + 1) * HEAD)
        co = conv[0, at].astype(F32)
        u = upd[0, at]
        st = step[0, h : h + 1]
        pair = gy[0, :, (h // 2) * 128 : (h // 2 + 1) * 128]
        both = jnp.concatenate([u, zero] if h % 2 == 0 else [zero, u], axis=0)
        score_grad = dot(pair, both)
        decay = jnp.exp2(cum_col[:, h : h + 1] - cum[h : h + 1] + bias)
        acc[...] += decay * score_grad
        score = (decay * gram).astype(BF16)
        gt = gyt[0, at]
        grad_u = dot(gt, score)
        y = dot(u, score, NT)
        gt = gt.astype(F32)
        row_sum = jnp.sum(gt * (y + rows_in[0, 1, h : h + 1] * statec[at]), axis=0, keepdims=True)
        col_sum = jnp.sum(u.astype(F32) * grad_u, axis=0, keepdims=True)
        cum_out = jnp.where(spot == h, row_sum - col_sum, cum_out)
        step_out = jnp.where(spot == h, jnp.sum(grad_u * co, axis=0, keepdims=True), step_out)
        skip_out = jnp.where(spot == h, jnp.sum(gt * co, axis=0, keepdims=True), skip_out)
        part[0, at] = (st * grad_u + skip[g, h] * gt).astype(BF16)
    heads_out[0, 0] = cum_out
    heads_out[0, 1] = step_out
    heads_out[0, 2] = skip_out
    grad_gram = acc[...].astype(BF16)
    scaled = jnp.concatenate(
        [
            (gyt[0, h * HEAD : (h + 1) * HEAD].astype(F32) * rows_in[0, 1, h : h + 1]).astype(BF16)
            for h in range(heads)
        ],
        axis=0,
    )
    gc[0] = (dot(grad_gram, bm[0]) + dot(scaled, state[0], TN)).astype(BF16)
    gb[0] = dot(grad_gram, cm[0], TN).astype(BF16)


def carry_kernel(
    index, rate, grad, bm, step, rows_in, heads_in, state, lagged, conv, slope, part, gb, gc,
    pay, grad_step, pre_out, edge, kept, sent, prods, scaled, tri,
):
    turn = pl.program_id(0)
    group = index[0] ^ turn

    @pl.when(turn == 0)
    def _():
        size = tri.shape
        tri[...] = (iota(size, 0) >= iota(size, 1)).astype(BF16)
    heads = step.shape[1]
    rows = step.shape[2]
    carry = dot(grad[0], bm[0], NT)
    spot = iota((heads, rows), 0)
    to_end = rows_in[0, 2]
    along = jnp.zeros((heads, rows), F32)
    inner = jnp.zeros((heads, 128), F32)
    for h in range(heads):
        at = slice(h * HEAD, (h + 1) * HEAD)
        cb = carry[at]
        st = step[0, h : h + 1]
        co = conv[0, at].astype(F32)
        along = jnp.where(spot == h, jnp.sum(cb * co, axis=0, keepdims=True), along)
        weight = st * to_end[h : h + 1]
        scaled[at] = (weight * co).astype(BF16)
        prod = grad[0, at].astype(F32) * state[0, at].astype(F32)
        inner = jnp.where(
            iota((heads, 128), 0) == h, jnp.sum(prod, axis=0, keepdims=True), inner
        )
        gp = part[0, at].astype(F32) + weight * cb
        gp = gp * slope[0, at].astype(F32)
        pre_out[0, at] = gp.astype(BF16)
        terms = [gp * lagged[0, j, at].astype(F32) for j in range(4)] + [gp]
        for j, term in enumerate(terms):
            lanes = slice(j % 2 * 128, j % 2 * 128 + 128)
            prods[j // 2, at, lanes] = (term[:, :128] + term[:, 128:]).astype(BF16)
        prods[2, at, 128:] = gp[:, :128].astype(BF16)
    total_b = (gb[0].astype(F32) + dot(scaled[...], grad[0], TN)).astype(BF16)
    for out, here in ((kept, turn < 2), (sent, turn >= 2)):

        @pl.when(here)
        def _():
            out[0, 0] = total_b
            out[0, 1] = gc[0]

    along = along * to_end
    step_two = along
    along = along * step[0]
    through = rows_in[0, 1][:, rows - 1 :]
    last = jnp.sum(along, axis=1, keepdims=True) + through * jnp.sum(inner, axis=1, keepdims=True)
    grad_cum = heads_in[0, 0] - along + jnp.where(iota((heads, rows), 1) == rows - 1, last, 0.0)
    grad_log = summed(grad_cum, tri[...])
    grad_step[0] = heads_in[0, 1] + step_two - per_head(rate, group, (heads, rows)) * grad_log
    spot = iota((ROWS + HALO, rows), 0)
    lane = iota((ROWS + HALO, rows), 1)
    total = jnp.zeros((ROWS, 128), F32)
    for i in range(prods.shape[1] // 128):
        at = slice(i * 128, (i + 1) * 128)
        for k in range(3):
            if k < 2:
                chosen = spot == i * 5 + 2 * k + (lane >= 128).astype(jnp.int32)
            else:
                chosen = spot == jnp.where(lane < 128, i * 5 + 4, ROWS + lane - 128)
            out = dot(chosen.astype(BF16), prods[k, at], NT)
            total = total + out[:ROWS]
        edge[0, :, at] = out[ROWS:].astype(BF16)
    few = jnp.concatenate([-step[0] * grad_log, heads_in[0, 2]], axis=0)
    upper = few.astype(BF16).astype(F32)
    few = jnp.concatenate([upper, few - upper], axis=1)
    few = jnp.concatenate([few, jnp.zeros((128 - 2 * heads, 2 * rows), F32)], axis=0).astype(BF16)
    total = total + dot((iota((ROWS, 2 * rows), 0) == 20).astype(BF16), few, NT)
    pay[:, 0, 0] = jnp.broadcast_to(total.astype(BF16), (pay.shape[0], ROWS, 128))


def input_kernel(first, lengths, pre, right, taps, out, here, away):
    rows = pre.shape[2]

    @pl.when(pl.program_id(0) == 0)
    def _():
        start = first[0]
        _, high = doc_bounds(start, lengths, rows)
        for j in range(1, 4):
            sub = iota((rows, rows), 0)
            lane = iota((rows, rows), 1)
            here[j - 1] = ((sub == lane + j) & (sub + start <= high)).astype(BF16)
            sub = iota((HALO, rows), 0) + rows
            lane = iota((HALO, rows), 1)
            away[j - 1] = ((sub == lane + j) & (sub + start <= high)).astype(F32)

    w = taps[0]
    total = w[:, 0:1] * pre[0].astype(F32)
    for j in range(1, 4):
        far = dot(right[0], away[j - 1].astype(BF16), TN)
        total = total + w[:, j : j + 1] * (dot(pre[0], here[j - 1]) + far)
    out[0] = jnp.transpose(total).astype(BF16)


def spread_kernel(parts, after, out):
    total = parts[0].astype(F32)
    for i in range(1, parts.shape[0]):
        total = total + parts[i].astype(F32)
    out[...] = jnp.broadcast_to(total.astype(out.dtype), out.shape)


def final_kernel(core, mine, other, weight, bias, rate, skip):
    each = mine.shape[0]
    heads = rate.shape[1]
    for g in range(bias.shape[0]):
        ours = core[0] == g // each
        rows = jnp.where(ours, mine[g % each], other[g % each])
        for i in range(bias.shape[1] // 128):
            at = slice(i * 128, (i + 1) * 128)
            for j in range(4):
                weight[j, g : g + 1, at] = rows[i * 5 + j : i * 5 + j + 1]
            bias[g : g + 1, at] = rows[i * 5 + 4 : i * 5 + 5]
        rate[g : g + 1] = rows[20:21, :heads]
        skip[g : g + 1] = rows[20:21, heads : 2 * heads]


def meet_kernel(kept, got, after, mine, passed):
    mine[...] = kept[0].astype(F32) + got[0].astype(F32)
    passed[...] = (kept[1].astype(F32) + got[1].astype(F32)).astype(BF16)


def pair_sum_kernel(mine, got, one, two):
    one[...] = mine[0] + got[0].astype(F32)
    two[...] = mine[1] + got[1].astype(F32)


def sum_kernel(parts, *refs):
    out = refs[-1]
    total = parts[0].astype(F32)
    for i in range(1, parts.shape[0]):
        total = total + parts[i].astype(F32)
    out[...] = total.astype(out.dtype)


ANY = pl.BlockSpec(memory_space=pl.ANY)
SMEM = pl.BlockSpec(memory_space=pltpu.SMEM)


def whole(shape):
    return pl.BlockSpec(shape, lambda *i: (0,) * len(shape))


def by_group(array, at=0):
    tail = tuple(array.shape[1:])
    return pl.BlockSpec((1,) + tail, lambda g: (g + at,) + (0,) * len(tail))


def array(shape, dtype):
    return jax.ShapeDtypeStruct(shape, dtype)


def in_hbm(a):
    return pltpu.with_memory_space_constraint(a, pltpu.HBM)


def call(kernel, grid, ins, outs, flops=0, nbytes=0, scratch=(), alias=None, mib=24):
    return pl.pallas_call(
        kernel,
        grid=grid,
        in_specs=[s for s, _ in ins],
        out_specs=[s for s, _ in outs],
        out_shape=[o for _, o in outs],
        scratch_shapes=list(scratch),
        input_output_aliases=alias or {},
        cost_estimate=pl.CostEstimate(flops=flops, bytes_accessed=nbytes, transcendentals=0),
        compiler_params=pltpu.CompilerParams(vmem_limit_bytes=mib * 1024 * 1024),
    )(*[a for _, a in ins])


def shifted(block, axis, distance):
    size = lax.axis_size(axis)
    route = [(i, i + distance) for i in range(size) if 0 <= i + distance < size]
    return lax.ppermute(block, axis, route)


def body(
    conv_input,
    output_grad,
    b_matrix,
    c_matrix,
    step_size,
    decay_rate,
    skip_gain,
    conv_weight,
    conv_bias,
    saved_state,
    doc_lengths,
):
    _, rows, groups, features = conv_input.shape
    heads = step_size.shape[3]
    blocks = lax.axis_size("context")
    first = (lax.axis_index("context") * rows).astype(jnp.int32).reshape(1)
    x = jnp.transpose(conv_input[0], (1, 0, 2))
    gy = jnp.transpose(output_grad[0], (1, 0, 2))
    bm = jnp.transpose(b_matrix[0], (1, 0, 2))
    cm = jnp.transpose(c_matrix[0], (1, 0, 2))
    step = jnp.transpose(step_size[0], (1, 2, 0))
    state = saved_state.reshape(groups, features, 128)
    taps = jnp.concatenate(
        [
            jnp.transpose(conv_weight, (1, 2, 0)),
            conv_bias[:, :, None],
            jnp.zeros((groups, features, 3), F32),
        ],
        axis=2,
    )
    sent = shifted(conv_input[0, rows - HALO :], "context", 1)
    halo = jnp.transpose(sent, (1, 0, 2))

    wide = array((groups, features, rows), BF16)
    per_row = array((groups, 3, heads, rows), F32)
    quads = [[q * groups + r for r in range(groups)] for q in range(blocks // groups)]
    size = features + EXTRA
    pay = array((groups, size, 128), BF16)
    count = len(quads)

    def owner(q, e):
        return q * groups + (e + (2 * q >= count)) % groups

    def to_earlier(block, distance):
        route = [
            (owner(q, e), owner(q - distance, e))
            for q in range(distance, count)
            for e in range(groups)
        ]
        return lax.ppermute(block, "context", route)

    shift = (lax.axis_index("context") * 2 >= blocks).astype(jnp.int32).reshape(1)

    def plain(a):
        tail = tuple(a.shape[1:])
        return pl.BlockSpec((1,) + tail, lambda g, i: (g,) + (0,) * len(tail))

    pay, gyt, rows_in = pl.pallas_call(
        offset_kernel,
        grid_spec=pltpu.PrefetchScalarGridSpec(
            num_scalar_prefetch=1,
            grid=(groups,),
            in_specs=[SMEM] * 3 + [plain(a) for a in (step, gy, cm)],
            out_specs=[
                pl.BlockSpec((1, size, 128), lambda g, i: ((g + i[0]) % groups, 0, 0)),
                plain(wide),
                plain(per_row),
            ],
            scratch_shapes=[pltpu.VMEM((rows, rows), BF16)],
        ),
        out_shape=[pay, wide, per_row],
        cost_estimate=pl.CostEstimate(flops=10**9, bytes_accessed=4 * 10**6, transcendentals=0),
        compiler_params=pltpu.CompilerParams(vmem_limit_bytes=60 * 1024 * 1024),
    )(shift, first, doc_lengths, decay_rate, step, gy, cm)

    def across(block, axis, among=None):
        return lax.all_to_all(block, axis, 0, 0, axis_index_groups=among, tiled=True)

    got = across(pay, "context", quads)
    quad = array((size, 128), BF16)
    (quad,) = call(
        quad_kernel,
        (),
        [(whole(got.shape), got)],
        [(whole(quad.shape), quad)],
        flops=10**7,
        nbytes=10**6,
    )
    near = to_earlier(quad, 1)
    far = to_earlier(quad, 2)
    masks = (pltpu.VMEM((3, rows, rows), BF16), pltpu.VMEM((3, HALO, rows), F32))
    lags = array((groups, 4, features, rows), BF16)
    lagged, conv, upd, slope = call(
        conv_kernel,
        (groups,),
        [(SMEM, first), (SMEM, doc_lengths)]
        + [(by_group(a), a) for a in (x, halo, step, taps)]
        + [(ANY, quad)],
        [(by_group(a), a) for a in (lags, wide, wide, wide)],
        flops=4 * 10**9,
        nbytes=10 * 10**6,
        mib=60,
        scratch=masks,
    )
    states = array((groups, features, 128), BF16)
    (states,) = call(
        scan_kernel,
        (),
        [(whole(a.shape), a) for a in (got, near, far)] + [(ANY, upd)],
        [(whole(states.shape), states)],
        flops=10**7,
        nbytes=10**6,
    )
    gram_out = array((groups, rows, 128), BF16)
    part, heads_in, gc, gb = call(
        intra_kernel,
        (groups,),
        [(SMEM, first), (SMEM, doc_lengths), (SMEM, skip_gain)]
        + [(by_group(a), a) for a in (conv, upd, gy, gyt, bm, cm, step, rows_in, state)]
        + [(ANY, states)],
        [(by_group(a), a) for a in (wide, per_row, gram_out, gram_out)],
        flops=16 * 10**9,
        nbytes=10 * 10**6,
        mib=60,
        scratch=(pltpu.VMEM((rows, rows), F32), pltpu.VMEM((features, rows), F32)),
    )
    grad = across(states, "context", quads)

    copies = lax.axis_size("dp")
    halves = 2 if copies % 2 == 0 else 1
    each = groups // halves
    parts = lax.axis_size("tensor")
    shares = array((copies // halves, halves, each, ROWS, 128), BF16)
    step_out = array((groups, heads, rows), F32)
    edges = array((groups, HALO, features), BF16)
    assert parts == groups == 4
    index = jnp.concatenate([lax.axis_index("tensor").astype(jnp.int32).reshape(1), shift])

    def turned(a):
        tail = tuple(a.shape[1:])
        return pl.BlockSpec((1,) + tail, lambda r, i: (i[0] ^ r,) + (0,) * len(tail))

    ins = (grad, bm, step, rows_in, heads_in, state, lagged, conv, slope, part, gb, gc)
    pair = (2, rows, 128)
    twice = array((2,) + pair, BF16)
    shared, grad_step, pre, edge, kept, sent = pl.pallas_call(
        carry_kernel,
        grid_spec=pltpu.PrefetchScalarGridSpec(
            num_scalar_prefetch=1,
            grid=(groups,),
            in_specs=[
                SMEM,
                pl.BlockSpec(
                    (1, features, 128), lambda r, i: (((i[0] ^ r) + i[1]) % groups, 0, 0)
                ),
            ]
            + [turned(a) for a in ins[1:]],
            out_specs=[
                pl.BlockSpec(
                    (copies // halves, 1, 1, ROWS, 128),
                    lambda r, i: (0, (i[0] ^ r) // each, (i[0] ^ r) % each, 0, 0),
                )
            ]
            + [turned(a) for a in (step_out, wide, edges)]
            + [
                pl.BlockSpec((1,) + pair, lambda r, i: (jnp.minimum(r, 1), 0, 0, 0)),
                pl.BlockSpec((1,) + pair, lambda r, i: (jnp.maximum(r - 2, 0), 0, 0, 0)),
            ],
            scratch_shapes=[
                pltpu.VMEM((3, features, rows), BF16),
                pltpu.VMEM((features, rows), BF16),
                pltpu.VMEM((rows, rows), BF16),
            ],
        ),
        out_shape=[shares, step_out, wide, edges, twice, twice],
        cost_estimate=pl.CostEstimate(flops=10**9, bytes_accessed=8 * 10**6, transcendentals=0),
        compiler_params=pltpu.CompilerParams(vmem_limit_bytes=60 * 1024 * 1024),
    )(index, decay_rate, *ins)

    def exchanged(block, bit):
        return lax.ppermute(block, "tensor", [(i, i ^ bit) for i in range(parts)])

    small = (each, ROWS, 128)
    shared = across(shared.reshape((copies,) + small), "dp")
    spread = array((blocks,) + small, BF16)
    right = shifted(edge, "context", -1)
    (shared,) = call(
        spread_kernel,
        (),
        [(whole(shared.shape), shared), (ANY, right)],
        [(whole(spread.shape), spread)],
    )
    natural = array((groups, rows, features), BF16)
    (grad_input,) = call(
        input_kernel,
        (groups,),
        [(SMEM, first), (SMEM, doc_lengths)] + [(by_group(a), a) for a in (in_hbm(pre), right, taps)],
        [(by_group(natural), natural)],
        flops=10**9,
        nbytes=4 * 10**6,
        scratch=(pltpu.VMEM((3, rows, rows), BF16), pltpu.VMEM((3, HALO, rows), F32)),
    )
    got = exchanged(sent, 2)
    part_out = array((rows, 128), F32)
    mine_b, passed = call(
        meet_kernel,
        (),
        [(whole(twice.shape), kept), (whole(twice.shape), got), (ANY, grad_input)],
        [(whole(pair), array(pair, F32)), (whole(pair), array(pair, BF16))],
    )
    shared = across(shared, "context")
    grad_b, grad_c = call(
        pair_sum_kernel,
        (),
        [(whole(pair), mine_b), (whole(pair), exchanged(passed, 1))],
        [(whole(part_out.shape), part_out)] * 2,
    )
    (mine,) = call(
        sum_kernel,
        (),
        [(whole(shared.shape), shared), (ANY, grad_input)],
        [(whole(small), array(small, F32))],
    )
    core = lax.axis_index("dp") % halves
    other = mine
    if halves == 2:
        other = lax.ppermute(mine, "dp", [(i, i ^ 1) for i in range(copies)])
    outs = [(4, groups, features), (groups, features), (groups, heads), (groups, heads)]
    weight, bias, rate, skip = call(
        final_kernel,
        (),
        [(SMEM, core.astype(jnp.int32).reshape(1)), (whole(small), mine), (whole(small), other)],
        [(whole(o), array(o, F32)) for o in outs],
    )
    return (
        jnp.transpose(grad_input, (1, 0, 2))[None],
        grad_b.reshape(1, rows, 1, 128),
        grad_c.reshape(1, rows, 1, 128),
        jnp.transpose(grad_step, (2, 0, 1))[None],
        weight,
        bias,
        rate,
        skip,
    )


def solution(mesh):
    return jax.shard_map(
        body,
        mesh=mesh,
        in_specs=(
            P("dp", "context", None, "tensor"),
            P("dp", "context", None, "tensor"),
            P("dp", "context", None, None),
            P("dp", "context", None, None),
            P("dp", "context", None, "tensor"),
            P(None, "tensor"),
            P(None, "tensor"),
            P(None, None, "tensor"),
            P(None, "tensor"),
            P("dp", "context", None, "tensor", None, None),
            P("dp", None),
        ),
        out_specs=(
            P("dp", "context", None, "tensor"),
            P("dp", "context", "tensor", None),
            P("dp", "context", "tensor", None),
            P("dp", "context", None, "tensor"),
            P(None, None, "tensor"),
            P(None, "tensor"),
            P(None, "tensor"),
            P(None, "tensor"),
        ),
        check_vma=False,
    )
```

```python
import functools

import jax
import jax.numpy as jnp
from jax import lax
from jax.experimental import pallas as pl
from jax.experimental.pallas import tpu as pltpu
from jax.sharding import PartitionSpec as P

F32 = jnp.float32
BF16 = jnp.bfloat16
LOG2E = 1.4426950408889634
FULL = lax.Precision.HIGHEST
HEAD = 64
HALO = 8
EXTRA = 16
ROWS = 24
FAR = 1 << 28


def dot(a, b, dims=((1,), (0,)), precision=None):
    return lax.dot_general(a, b, (dims, ((), ())), precision=precision, preferred_element_type=F32)


NT = ((1,), (1,))
TN = ((0,), (0,))


def iota(shape, axis):
    return lax.broadcasted_iota(jnp.int32, shape, axis)


def doc_bounds(first, lengths, rows):
    pos = first + iota((1, rows), 1)
    low = jnp.zeros((1, rows), jnp.int32)
    high = jnp.full((1, rows), FAR, jnp.int32)
    start = jnp.int32(0)
    for d in range(lengths.shape[1]):
        low = jnp.where(pos >= start, start, low)
        start = start + lengths[0, d]
        high = jnp.minimum(high, jnp.where(start > pos, start - 1, FAR))
    return low, high


def per_head(values, group, shape):
    column = jnp.zeros(shape, F32)
    for h in range(shape[0]):
        column = jnp.where(iota(shape, 0) == h, values[group, h], column)
    return column


def summed(values, chosen):
    count = values.shape[0]
    upper = values.astype(BF16).astype(F32)
    rest = values - upper
    middle = rest.astype(BF16).astype(F32)
    parts = jnp.concatenate([upper, middle, rest - middle], axis=0).astype(BF16)
    out = dot(parts, chosen)
    return out[:count] + out[count : 2 * count] + out[2 * count :]


def offset_kernel(shift, first, lengths, rate, step, gy, cm, pay, gyt, rows_out, tri):
    g = pl.program_id(0)

    @pl.when(g == 0)
    def _():
        size = tri.shape
        tri[...] = (iota(size, 0) <= iota(size, 1)).astype(BF16)

    rows = step.shape[2]
    heads = step.shape[1]
    low, high = doc_bounds(first[0], lengths, rows)
    cum = summed(step[0] * (per_head(rate, g, (heads, rows)) * (-LOG2E)), tri[...])
    from_start = jnp.where(low < first[0], jnp.exp2(cum), 0.0)
    last = jnp.broadcast_to(cum[:, rows - 1 :], (heads, rows))
    to_end = jnp.where(high >= first[0] + rows - 1, jnp.exp2(jnp.minimum(last - cum, 0.0)), 0.0)
    rows_out[0, 0] = cum
    rows_out[0, 1] = from_start
    rows_out[0, 2] = to_end
    gt = jnp.transpose(gy[0])
    gyt[0] = gt
    gt = gt.astype(F32)
    scaled = jnp.concatenate(
        [gt[h * HEAD : (h + 1) * HEAD] * from_start[h : h + 1] for h in range(heads)], axis=0
    ).astype(BF16)
    pay[0, : heads * HEAD] = dot(scaled, cm[0]).astype(BF16)
    pay[0, heads * HEAD :] = factors_out(jnp.broadcast_to(from_start[:, rows - 1 :], (heads, 128)))


def factors_out(values):
    upper = values.astype(BF16).astype(F32)
    return jnp.concatenate([upper, values - upper], axis=0).astype(BF16)


def factors_in(rows):
    rows = rows.astype(F32)
    half = rows.shape[0] // 2
    return rows[:half] + rows[half:]


def quad_kernel(got, out):
    count = got.shape[0]
    size = got.shape[1] - EXTRA
    through = [factors_in(got[r, size:]) for r in range(count)]
    total = through[0]
    for r in range(1, count):
        total = total * through[r]
    for h in range(size // HEAD):
        at = slice(h * HEAD, (h + 1) * HEAD)
        state = got[count - 1, at].astype(F32)
        for r in range(count - 2, -1, -1):
            state = through[r][h : h + 1] * state + got[r, at].astype(F32)
        out[at] = state.astype(BF16)
    out[size:] = factors_out(total)


def scan_kernel(got, near, far, after, out):
    count = got.shape[0]
    size = got.shape[1] - EXTRA
    through = [factors_in(got[r, size:]) for r in range(count)]
    total = factors_in(near[size:])
    for h in range(size // HEAD):
        at = slice(h * HEAD, (h + 1) * HEAD)
        state = near[at].astype(F32) + total[h : h + 1] * far[at].astype(F32)
        out[count - 1, at] = state.astype(BF16)
        for r in range(count - 2, -1, -1):
            state = through[r + 1][h : h + 1] * state + got[r + 1, at].astype(F32)
            out[r, at] = state.astype(BF16)


def lag_masks(first, lengths, here, away):
    rows = here.shape[2]
    start = first[0]
    low, _ = doc_bounds(start, lengths, rows)
    for j in range(1, 4):
        sub = iota((rows, rows), 0)
        lane = iota((rows, rows), 1)
        here[j - 1] = ((sub + j == lane) & (sub + start >= low)).astype(BF16)
        sub = iota((HALO, rows), 0) - HALO
        lane = iota((HALO, rows), 1)
        away[j - 1] = ((sub + j == lane) & (sub + start >= low)).astype(F32)


def lag(xt, halo, here, away, j):
    return dot(xt, here[j - 1]) + dot(halo, away[j - 1].astype(BF16), TN)


def conv_kernel(
    first, lengths, x, halo, step, taps, after, lagged, conv, upd, slope, here, away
):
    heads = step.shape[1]

    @pl.when(pl.program_id(0) == 0)
    def _():
        lag_masks(first, lengths, here, away)

    xt = jnp.transpose(x[0])
    lagged[0, 0] = xt
    for j in range(1, 4):
        lagged[0, j] = lag(xt, halo[0], here, away, j).astype(BF16)
    for h in range(heads):
        at = slice(h * HEAD, (h + 1) * HEAD)
        w = taps[0, at]
        pre = w[:, 4:5] + w[:, 0:1] * lagged[0, 0, at].astype(F32)
        for j in range(1, 4):
            pre = pre + w[:, j : j + 1] * lagged[0, j, at].astype(F32)
        sig = 1.0 / (1.0 + jnp.exp(-pre))
        co = (pre * sig).astype(BF16)
        conv[0, at] = co
        slope[0, at] = (sig * (1.0 + pre * (1.0 - sig))).astype(BF16)
        upd[0, at] = (step[0, h : h + 1] * co.astype(F32)).astype(BF16)


def intra_kernel(
    first, lengths, skip, conv, upd, gy, gyt, bm, cm, step, rows_in, state, after,
    part, heads_out, gc, gb, acc, statec,
):
    g = pl.program_id(0)
    heads = step.shape[1]
    rows = step.shape[2]
    start = first[0]
    _, high = doc_bounds(start, lengths, rows)
    sub = iota((rows, rows), 0)
    lane = iota((rows, rows), 1)
    statec[...] = dot(state[0], cm[0], NT)
    gram = dot(cm[0], bm[0], NT)
    bias = jnp.where((sub >= lane) & (sub + start <= high), 0.0, -1e30)
    cum = rows_in[0, 0]
    cum_col = jnp.transpose(cum)
    acc[...] = jnp.zeros((rows, rows), F32)
    zero = jnp.zeros((HEAD, rows), BF16)
    spot = iota((heads, rows), 0)
    cum_out = jnp.zeros((heads, rows), F32)
    step_out = jnp.zeros((heads, rows), F32)
    skip_out = jnp.zeros((heads, rows), F32)
    for h in range(heads):
        at = slice(h * HEAD, (h + 1) * HEAD)
        co = conv[0, at].astype(F32)
        u = upd[0, at]
        st = step[0, h : h + 1]
        pair = gy[0, :, (h // 2) * 128 : (h // 2 + 1) * 128]
        both = jnp.concatenate([u, zero] if h % 2 == 0 else [zero, u], axis=0)
        score_grad = dot(pair, both)
        decay = jnp.exp2(cum_col[:, h : h + 1] - cum[h : h + 1] + bias)
        acc[...] += decay * score_grad
        score = (decay * gram).astype(BF16)
        gt = gyt[0, at]
        grad_u = dot(gt, score)
        y = dot(u, score, NT)
        gt = gt.astype(F32)
        row_sum = jnp.sum(gt * (y + rows_in[0, 1, h : h + 1] * statec[at]), axis=0, keepdims=True)
        col_sum = jnp.sum(u.astype(F32) * grad_u, axis=0, keepdims=True)
        cum_out = jnp.where(spot == h, row_sum - col_sum, cum_out)
        step_out = jnp.where(spot == h, jnp.sum(grad_u * co, axis=0, keepdims=True), step_out)
        skip_out = jnp.where(spot == h, jnp.sum(gt * co, axis=0, keepdims=True), skip_out)
        part[0, at] = (st * grad_u + skip[g, h] * gt).astype(BF16)
    heads_out[0, 0] = cum_out
    heads_out[0, 1] = step_out
    heads_out[0, 2] = skip_out
    grad_gram = acc[...].astype(BF16)
    scaled = jnp.concatenate(
        [
            (gyt[0, h * HEAD : (h + 1) * HEAD].astype(F32) * rows_in[0, 1, h : h + 1]).astype(BF16)
            for h in range(heads)
        ],
        axis=0,
    )
    gc[0] = (dot(grad_gram, bm[0]) + dot(scaled, state[0], TN)).astype(BF16)
    gb[0] = dot(grad_gram, cm[0], TN).astype(BF16)


def carry_kernel(
    index, rate, grad, bm, step, rows_in, heads_in, state, lagged, conv, slope, part, gb, gc,
    pay, grad_step, pre_out, edge, kept, sent, prods, scaled, tri,
):
    turn = pl.program_id(0)
    group = index[0] ^ turn

    @pl.when(turn == 0)
    def _():
        size = tri.shape
        tri[...] = (iota(size, 0) >= iota(size, 1)).astype(BF16)
    heads = step.shape[1]
    rows = step.shape[2]
    carry = dot(grad[0], bm[0], NT)
    spot = iota((heads, rows), 0)
    to_end = rows_in[0, 2]
    along = jnp.zeros((heads, rows), F32)
    inner = jnp.zeros((heads, 128), F32)
    for h in range(heads):
        at = slice(h * HEAD, (h + 1) * HEAD)
        cb = carry[at]
        st = step[0, h : h + 1]
        co = conv[0, at].astype(F32)
        along = jnp.where(spot == h, jnp.sum(cb * co, axis=0, keepdims=True), along)
        weight = st * to_end[h : h + 1]
        scaled[at] = (weight * co).astype(BF16)
        prod = grad[0, at].astype(F32) * state[0, at].astype(F32)
        inner = jnp.where(
            iota((heads, 128), 0) == h, jnp.sum(prod, axis=0, keepdims=True), inner
        )
        gp = part[0, at].astype(F32) + weight * cb
        gp = gp * slope[0, at].astype(F32)
        pre_out[0, at] = gp.astype(BF16)
        terms = [gp * lagged[0, j, at].astype(F32) for j in range(4)] + [gp]
        for j, term in enumerate(terms):
            lanes = slice(j % 2 * 128, j % 2 * 128 + 128)
            prods[j // 2, at, lanes] = (term[:, :128] + term[:, 128:]).astype(BF16)
        prods[2, at, 128:] = gp[:, :128].astype(BF16)
    total_b = (gb[0].astype(F32) + dot(scaled[...], grad[0], TN)).astype(BF16)
    for out, here in ((kept, turn < 2), (sent, turn >= 2)):

        @pl.when(here)
        def _():
            out[0, 0] = total_b
            out[0, 1] = gc[0]

    along = along * to_end
    step_two = along
    along = along * step[0]
    through = rows_in[0, 1][:, rows - 1 :]
    last = jnp.sum(along, axis=1, keepdims=True) + through * jnp.sum(inner, axis=1, keepdims=True)
    grad_cum = heads_in[0, 0] - along + jnp.where(iota((heads, rows), 1) == rows - 1, last, 0.0)
    grad_log = summed(grad_cum, tri[...])
    grad_step[0] = heads_in[0, 1] + step_two - per_head(rate, group, (heads, rows)) * grad_log
    spot = iota((ROWS + HALO, rows), 0)
    lane = iota((ROWS + HALO, rows), 1)
    total = jnp.zeros((ROWS, 128), F32)
    for i in range(prods.shape[1] // 128):
        at = slice(i * 128, (i + 1) * 128)
        for k in range(3):
            if k < 2:
                chosen = spot == i * 5 + 2 * k + (lane >= 128).astype(jnp.int32)
            else:
                chosen = spot == jnp.where(lane < 128, i * 5 + 4, ROWS + lane - 128)
            out = dot(chosen.astype(BF16), prods[k, at], NT)
            total = total + out[:ROWS]
        edge[0, :, at] = out[ROWS:].astype(BF16)
    few = jnp.concatenate([-step[0] * grad_log, heads_in[0, 2]], axis=0)
    upper = few.astype(BF16).astype(F32)
    few = jnp.concatenate([upper, few - upper], axis=1)
    few = jnp.concatenate([few, jnp.zeros((128 - 2 * heads, 2 * rows), F32)], axis=0).astype(BF16)
    total = total + dot((iota((ROWS, 2 * rows), 0) == 20).astype(BF16), few, NT)
    pay[:, 0, 0] = jnp.broadcast_to(total.astype(BF16), (pay.shape[0], ROWS, 128))


def input_kernel(first, lengths, pre, right, taps, out, here, away):
    rows = pre.shape[2]

    @pl.when(pl.program_id(0) == 0)
    def _():
        start = first[0]
        _, high = doc_bounds(start, lengths, rows)
        for j in range(1, 4):
            sub = iota((rows, rows), 0)
            lane = iota((rows, rows), 1)
            here[j - 1] = ((sub == lane + j) & (sub + start <= high)).astype(BF16)
            sub = iota((HALO, rows), 0) + rows
            lane = iota((HALO, rows), 1)
            away[j - 1] = ((sub == lane + j) & (sub + start <= high)).astype(F32)

    w = taps[0]
    total = w[:, 0:1] * pre[0].astype(F32)
    for j in range(1, 4):
        far = dot(right[0], away[j - 1].astype(BF16), TN)
        total = total + w[:, j : j + 1] * (dot(pre[0], here[j - 1]) + far)
    out[0] = jnp.transpose(total.astype(BF16))


def spread_kernel(parts, after, out):
    total = parts[0].astype(F32)
    for i in range(1, parts.shape[0]):
        total = total + parts[i].astype(F32)
    out[...] = jnp.broadcast_to(total.astype(out.dtype), out.shape)


def final_kernel(core, mine, other, weight, bias, rate, skip):
    each = mine.shape[0]
    heads = rate.shape[1]
    for g in range(bias.shape[0]):
        ours = core[0] == g // each
        rows = jnp.where(ours, mine[g % each], other[g % each])
        for i in range(bias.shape[1] // 128):
            at = slice(i * 128, (i + 1) * 128)
            for j in range(4):
                weight[j, g : g + 1, at] = rows[i * 5 + j : i * 5 + j + 1]
            bias[g : g + 1, at] = rows[i * 5 + 4 : i * 5 + 5]
        rate[g : g + 1] = rows[20:21, :heads]
        skip[g : g + 1] = rows[20:21, heads : 2 * heads]


def meet_kernel(kept, got, after, mine, passed):
    mine[...] = kept[0].astype(F32) + got[0].astype(F32)
    passed[...] = (kept[1].astype(F32) + got[1].astype(F32)).astype(BF16)


def pair_sum_kernel(mine, got, one, two):
    one[...] = mine[0] + got[0].astype(F32)
    two[...] = mine[1] + got[1].astype(F32)


def sum_kernel(parts, *refs):
    out = refs[-1]
    total = parts[0].astype(F32)
    for i in range(1, parts.shape[0]):
        total = total + parts[i].astype(F32)
    out[...] = total.astype(out.dtype)


ANY = pl.BlockSpec(memory_space=pl.ANY)
SMEM = pl.BlockSpec(memory_space=pltpu.SMEM)


def whole(shape):
    return pl.BlockSpec(shape, lambda *i: (0,) * len(shape))


def by_group(array, at=0):
    tail = tuple(array.shape[1:])
    return pl.BlockSpec((1,) + tail, lambda g: (g + at,) + (0,) * len(tail))


def array(shape, dtype):
    return jax.ShapeDtypeStruct(shape, dtype)


def in_hbm(a):
    return pltpu.with_memory_space_constraint(a, pltpu.HBM)


def call(kernel, grid, ins, outs, flops=0, nbytes=0, scratch=(), alias=None, mib=24):
    return pl.pallas_call(
        kernel,
        grid=grid,
        in_specs=[s for s, _ in ins],
        out_specs=[s for s, _ in outs],
        out_shape=[o for _, o in outs],
        scratch_shapes=list(scratch),
        input_output_aliases=alias or {},
        cost_estimate=pl.CostEstimate(flops=flops, bytes_accessed=nbytes, transcendentals=0),
        compiler_params=pltpu.CompilerParams(vmem_limit_bytes=mib * 1024 * 1024),
    )(*[a for _, a in ins])


def shifted(block, axis, distance):
    size = lax.axis_size(axis)
    route = [(i, i + distance) for i in range(size) if 0 <= i + distance < size]
    return lax.ppermute(block, axis, route)


def body(
    conv_input,
    output_grad,
    b_matrix,
    c_matrix,
    step_size,
    decay_rate,
    skip_gain,
    conv_weight,
    conv_bias,
    saved_state,
    doc_lengths,
):
    _, rows, groups, features = conv_input.shape
    heads = step_size.shape[3]
    blocks = lax.axis_size("context")
    first = (lax.axis_index("context") * rows).astype(jnp.int32).reshape(1)
    x = jnp.transpose(conv_input[0], (1, 0, 2))
    gy = jnp.transpose(output_grad[0], (1, 0, 2))
    bm = jnp.transpose(b_matrix[0], (1, 0, 2))
    cm = jnp.transpose(c_matrix[0], (1, 0, 2))
    step = jnp.transpose(step_size[0], (1, 2, 0))
    state = saved_state.reshape(groups, features, 128)
    taps = jnp.concatenate(
        [
            jnp.transpose(conv_weight, (1, 2, 0)),
            conv_bias[:, :, None],
            jnp.zeros((groups, features, 3), F32),
        ],
        axis=2,
    )
    sent = shifted(conv_input[0, rows - HALO :], "context", 1)
    halo = jnp.transpose(sent, (1, 0, 2))

    wide = array((groups, features, rows), BF16)
    per_row = array((groups, 3, heads, rows), F32)
    quads = [[q * groups + r for r in range(groups)] for q in range(blocks // groups)]
    size = features + EXTRA
    pay = array((groups, size, 128), BF16)
    count = len(quads)

    def owner(q, e):
        return q * groups + (e + (2 * q >= count)) % groups

    def to_earlier(block, distance):
        route = [
            (owner(q, e), owner(q - distance, e))
            for q in range(distance, count)
            for e in range(groups)
        ]
        return lax.ppermute(block, "context", route)

    shift = (lax.axis_index("context") * 2 >= blocks).astype(jnp.int32).reshape(1)

    def plain(a):
        tail = tuple(a.shape[1:])
        return pl.BlockSpec((1,) + tail, lambda g, i: (g,) + (0,) * len(tail))

    pay, gyt, rows_in = pl.pallas_call(
        offset_kernel,
        grid_spec=pltpu.PrefetchScalarGridSpec(
            num_scalar_prefetch=1,
            grid=(groups,),
            in_specs=[SMEM] * 3 + [plain(a) for a in (step, gy, cm)],
            out_specs=[
                pl.BlockSpec((1, size, 128), lambda g, i: ((g + i[0]) & (groups - 1), 0, 0)),
                plain(wide),
                plain(per_row),
            ],
            scratch_shapes=[pltpu.VMEM((rows, rows), BF16)],
        ),
        out_shape=[pay, wide, per_row],
        cost_estimate=pl.CostEstimate(flops=10**9, bytes_accessed=4 * 10**6, transcendentals=0),
        compiler_params=pltpu.CompilerParams(vmem_limit_bytes=60 * 1024 * 1024),
    )(shift, first, doc_lengths, decay_rate, step, gy, cm)

    def across(block, axis, among=None):
        return lax.all_to_all(block, axis, 0, 0, axis_index_groups=among, tiled=True)

    got = across(pay, "context", quads)
    quad = array((size, 128), BF16)
    (quad,) = call(
        quad_kernel,
        (),
        [(whole(got.shape), got)],
        [(whole(quad.shape), quad)],
        flops=10**7,
        nbytes=10**6,
    )
    near = to_earlier(quad, 1)
    far = to_earlier(quad, 2)
    masks = (pltpu.VMEM((3, rows, rows), BF16), pltpu.VMEM((3, HALO, rows), F32))
    lags = array((groups, 4, features, rows), BF16)
    lagged, conv, upd, slope = call(
        conv_kernel,
        (groups,),
        [(SMEM, first), (SMEM, doc_lengths)]
        + [(by_group(a), a) for a in (x, halo, step, taps)]
        + [(ANY, quad)],
        [(by_group(a), a) for a in (lags, wide, wide, wide)],
        flops=4 * 10**9,
        nbytes=10 * 10**6,
        mib=60,
        scratch=masks,
    )
    states = array((groups, features, 128), BF16)
    (states,) = call(
        scan_kernel,
        (),
        [(whole(a.shape), a) for a in (got, near, far)] + [(ANY, in_hbm(upd))],
        [(whole(states.shape), states)],
        flops=10**7,
        nbytes=10**6,
    )
    gram_out = array((groups, rows, 128), BF16)
    part, heads_in, gc, gb = call(
        intra_kernel,
        (groups,),
        [(SMEM, first), (SMEM, doc_lengths), (SMEM, skip_gain)]
        + [(by_group(a), a) for a in (conv, upd, gy, gyt, bm, cm, step, rows_in, state)]
        + [(ANY, states)],
        [(by_group(a), a) for a in (wide, per_row, gram_out, gram_out)],
        flops=16 * 10**9,
        nbytes=10 * 10**6,
        mib=60,
        scratch=(pltpu.VMEM((rows, rows), F32), pltpu.VMEM((features, rows), F32)),
    )
    grad = across(states, "context", quads)

    copies = lax.axis_size("dp")
    halves = 2 if copies % 2 == 0 else 1
    each = groups // halves
    parts = lax.axis_size("tensor")
    shares = array((copies // halves, halves, each, ROWS, 128), BF16)
    step_out = array((groups, heads, rows), F32)
    edges = array((groups, HALO, features), BF16)
    assert parts == groups == 4 and each & (each - 1) == 0
    shift_each = each.bit_length() - 1
    index = jnp.concatenate([lax.axis_index("tensor").astype(jnp.int32).reshape(1), shift])

    def turned(a):
        tail = tuple(a.shape[1:])
        return pl.BlockSpec((1,) + tail, lambda r, i: (i[0] ^ r,) + (0,) * len(tail))

    ins = (grad, bm, step, rows_in, heads_in, state, lagged, conv, slope, part, gb, gc)
    pair = (2, rows, 128)
    twice = array((2,) + pair, BF16)
    shared, grad_step, pre, edge, kept, sent = pl.pallas_call(
        carry_kernel,
        grid_spec=pltpu.PrefetchScalarGridSpec(
            num_scalar_prefetch=1,
            grid=(groups,),
            in_specs=[
                SMEM,
                pl.BlockSpec(
                    (1, features, 128), lambda r, i: (((i[0] ^ r) + i[1]) & (groups - 1), 0, 0)
                ),
            ]
            + [turned(a) for a in ins[1:]],
            out_specs=[
                pl.BlockSpec(
                    (copies // halves, 1, 1, ROWS, 128),
                    lambda r, i: (0, (i[0] ^ r) >> shift_each, (i[0] ^ r) & (each - 1), 0, 0),
                )
            ]
            + [turned(a) for a in (step_out, wide, edges)]
            + [
                pl.BlockSpec((1,) + pair, lambda r, i: (jnp.minimum(r, 1), 0, 0, 0)),
                pl.BlockSpec((1,) + pair, lambda r, i: (jnp.maximum(r - 2, 0), 0, 0, 0)),
            ],
            scratch_shapes=[
                pltpu.VMEM((3, features, rows), BF16),
                pltpu.VMEM((features, rows), BF16),
                pltpu.VMEM((rows, rows), BF16),
            ],
        ),
        out_shape=[shares, step_out, wide, edges, twice, twice],
        cost_estimate=pl.CostEstimate(flops=10**9, bytes_accessed=8 * 10**6, transcendentals=0),
        compiler_params=pltpu.CompilerParams(vmem_limit_bytes=60 * 1024 * 1024),
    )(index, decay_rate, *ins)

    def exchanged(block, bit):
        return lax.ppermute(block, "tensor", [(i, i ^ bit) for i in range(parts)])

    small = (each, ROWS, 128)
    shared = across(shared.reshape((copies,) + small), "dp")
    spread = array((blocks,) + small, BF16)
    right = shifted(edge, "context", -1)
    (shared,) = call(
        spread_kernel,
        (),
        [(whole(shared.shape), shared), (ANY, right)],
        [(whole(spread.shape), spread)],
    )
    natural = array((groups, rows, features), BF16)
    (grad_input,) = call(
        input_kernel,
        (groups,),
        [(SMEM, first), (SMEM, doc_lengths)] + [(by_group(a), a) for a in (pre, right, taps)],
        [(by_group(natural), natural)],
        flops=10**9,
        nbytes=4 * 10**6,
        scratch=(pltpu.VMEM((3, rows, rows), BF16), pltpu.VMEM((3, HALO, rows), F32)),
    )
    got = exchanged(sent, 2)
    part_out = array((rows, 128), F32)
    mine_b, passed = call(
        meet_kernel,
        (),
        [(whole(twice.shape), kept), (whole(twice.shape), got), (ANY, grad_input)],
        [(whole(pair), array(pair, F32)), (whole(pair), array(pair, BF16))],
    )
    shared = across(shared, "context")
    grad_b, grad_c = call(
        pair_sum_kernel,
        (),
        [(whole(pair), mine_b), (whole(pair), exchanged(passed, 1))],
        [(whole(part_out.shape), part_out)] * 2,
    )
    (mine,) = call(
        sum_kernel,
        (),
        [(whole(shared.shape), shared), (ANY, grad_input)],
        [(whole(small), array(small, F32))],
    )
    core = lax.axis_index("dp") % halves
    other = mine
    if halves == 2:
        other = lax.ppermute(mine, "dp", [(i, i ^ 1) for i in range(copies)])
    outs = [(4, groups, features), (groups, features), (groups, heads), (groups, heads)]
    weight, bias, rate, skip = call(
        final_kernel,
        (),
        [(SMEM, core.astype(jnp.int32).reshape(1)), (whole(small), mine), (whole(small), other)],
        [(whole(o), array(o, F32)) for o in outs],
    )
    return (
        jnp.transpose(grad_input, (1, 0, 2))[None],
        grad_b.reshape(1, rows, 1, 128),
        grad_c.reshape(1, rows, 1, 128),
        jnp.transpose(grad_step, (2, 0, 1))[None],
        weight,
        bias,
        rate,
        skip,
    )


def solution(mesh):
    return jax.shard_map(
        body,
        mesh=mesh,
        in_specs=(
            P("dp", "context", None, "tensor"),
            P("dp", "context", None, "tensor"),
            P("dp", "context", None, None),
            P("dp", "context", None, None),
            P("dp", "context", None, "tensor"),
            P(None, "tensor"),
            P(None, "tensor"),
            P(None, None, "tensor"),
            P(None, "tensor"),
            P("dp", "context", None, "tensor", None, None),
            P("dp", None),
        ),
        out_specs=(
            P("dp", "context", None, "tensor"),
            P("dp", "context", "tensor", None),
            P("dp", "context", "tensor", None),
            P("dp", "context", None, "tensor"),
            P(None, None, "tensor"),
            P(None, "tensor"),
            P(None, "tensor"),
            P(None, "tensor"),
        ),
        check_vma=False,
    )
```
